512 devices in a mesh: frames: 64 (over z, y_hi, core), rows: 8 (over x, y_lo).
Axes of the slice: x: 4, y: 4 (y_hi: 2, y_lo: 2; y = y_hi * 2 + y_lo), z: 16, core: 2. Of those that a mesh axis runs over, the one named last changes fastest.
Arguments:
- coarse_features: bfloat16 [64, 16, 24, 256], P('frames', 'rows'), may hold values from -64 to 64
- fine_features: bfloat16 [64, 64, 96, 128], P('frames', 'rows'), may hold values from -96 to 96
- coarse_weight: bfloat16 [256, 256], replicated, may hold values from -0.375 to 0.375
- fine_weight: bfloat16 [128, 128], replicated, may hold values from -0.5 to 0.5
- grad_refined: float32 [64, 2, 6144], P('frames', None, 'rows'), may hold values from -24 to 24
- grad_back: float32 [64, 2, 384], P('frames', None, 'rows'), may hold values from -192 to 192
Outputs:
- coarse_grad: bfloat16 [64, 16, 24, 256], P('frames', 'rows')
- fine_grad: bfloat16 [64, 64, 96, 128], P('frames', 'rows')
- coarse_weight_grad: float32 [256, 256], replicated
- fine_weight_grad: float32 [128, 128], replicated
The draws below stay inside these ranges and needn't reach their ends.
All inputs are finite; a program needn't handle non-finite values.
Results may differ from the reference program's by a relative error of at most 0.007.
The reference program's roundings to bfloat16 on the way count: a program that leaves them out, or rounds other values in their place, can miss the bound.
Values may be sent and summed in bfloat16 or wider, within the bound.
No kernel may reach another device: no remote copies, remote signals or barrier semaphores. Data moves between devices by JAX's collectives and lax.ppermute only.
A program may use at most 64 MiB of HBM per device.

```python
import math
import jax
import jax.numpy as jnp
from jax import lax

C = 256
FC = 128
W = 24
H = 16
HF = 64
WF = 96
HF_DEV = 8
PAIRS = 64


def draw_coarse_features(key, part):
    key = jax.random.fold_in(key, 11)
    noise_key = jax.random.fold_in(key, 0)
    positions = H * W
    noise_base = jnp.clip(jax.random.normal(noise_key, (PAIRS, positions, C), jnp.float32), -4.0, 4.0)
    values = noise_base
    return values.reshape(PAIRS, H, W, C).astype(jnp.bfloat16)


def draw_fine_features(key, part):
    key = jax.random.fold_in(key, 23)
    noise_key = jax.random.fold_in(key, 0)
    positions = HF * WF
    noise_base = jnp.clip(jax.random.normal(noise_key, (PAIRS, positions, FC), jnp.float32), -4.0, 4.0)
    values = noise_base
    return values.reshape(PAIRS, HF, WF, FC).astype(jnp.bfloat16)


def levels(stream_key, extent, cuts, least, high):
    def one(dim, shards_of):
        heights = jax.random.uniform(jax.random.fold_in(jax.random.fold_in(stream_key, 6), dim), (shards_of,), jnp.float32, least / len(cuts), high / len(cuts))
        return jnp.repeat(jnp.exp(heights), extent[dim] // shards_of).reshape((-1,) + (1,) * (len(extent) - dim - 1))

    factor_of = one(*cuts[0])
    for cut in cuts[1:]:
        factor_of = factor_of * one(*cut)
    return factor_of


def gaussian(stream_key, dims, scale, reach, cuts=(), kind=jnp.bfloat16):
    loudness = levels(stream_key, dims, cuts, -0.22, 0.18) if cuts else 1.0
    result = jax.random.normal(stream_key, dims, jnp.float32) * scale * loudness
    return jnp.minimum(jnp.maximum(result, -reach), reach).astype(kind)


def setup_inputs(seed: int = 0) -> dict:
    streams_of = jax.random.split(jax.random.key(seed), 7)
    return {
        "coarse_features": draw_coarse_features(jax.random.fold_in(streams_of[6], 71), 0),
        "fine_features": draw_fine_features(jax.random.fold_in(streams_of[6], 71), 0),
        "coarse_weight": gaussian(streams_of[2], (C, C), C ** -0.5, 0.375),
        "fine_weight": gaussian(streams_of[3], (FC, FC), FC ** -0.5, 0.5),
        "grad_refined": gaussian(streams_of[4], (PAIRS, 2, HF * WF), 4.0, 24.0, ((0, 64), (2, 8)), jnp.float32),
        "grad_back": gaussian(streams_of[5], (PAIRS, 2, H * W), 32.0, 192.0, ((0, 64), (2, 8)), jnp.float32),
    }


def project(frame, weight):
    return jnp.dot(frame, weight, preferred_element_type=jnp.float32).astype(jnp.bfloat16)

def attend(queries, key_rows, coord_x, coord_y):
    channels = queries.shape[1]
    scores = jnp.dot(queries, key_rows.T, preferred_element_type=jnp.float32) / math.sqrt(channels)
    row_top = lax.optimization_barrier(jnp.max(scores, axis=1))
    exponent = jnp.exp(scores - row_top[:, None])
    totals = lax.optimization_barrier(jnp.sum(exponent, axis=1))
    chances = exponent / totals[:, None]
    mean_x = jnp.dot(chances, coord_x, precision=lax.Precision.HIGHEST)
    mean_y = jnp.dot(chances, coord_y, precision=lax.Precision.HIGHEST)
    return (chances, row_top, totals, mean_x, mean_y)

def weigh(chances, cot_x, cot_y, mean_x, mean_y, coord_x, coord_y, channels):
    spread = cot_x[:, None] * coord_x[None, :] + cot_y[:, None] * coord_y[None, :]
    centre = cot_x * mean_x + cot_y * mean_y
    return (chances * (spread - centre[:, None]) / math.sqrt(channels)).astype(jnp.bfloat16)

def fine_pair(queries, key_frame, grad_x, grad_y):
    height, columns, channels = queries.shape
    root_depth = math.sqrt(channels)
    padded = jnp.pad(key_frame, ((4, 4), (4, 4), (0, 0))).astype(jnp.float32)
    query_wide = queries.astype(jnp.float32)
    shifts = [(row_step, col_step) for row_step in range(-4, 5) for col_step in range(-4, 5)]
    scores = jnp.stack([lax.optimization_barrier(jnp.sum(query_wide * padded[4 + row_step:4 + row_step + height, 4 + col_step:4 + col_step + columns], axis=-1)) for row_step, col_step in shifts]) / root_depth
    steps_axis = jnp.arange(9, dtype=jnp.float32) - 4.0
    shift_y = jnp.repeat(steps_axis, 9)[:, None, None]
    shift_x = jnp.tile(steps_axis, 9)[:, None, None]
    row_top = lax.optimization_barrier(jnp.max(scores, axis=0, keepdims=True))
    exponent = jnp.exp(scores - row_top)
    chances = exponent / lax.optimization_barrier(jnp.sum(exponent, axis=0, keepdims=True))
    mean_x = lax.optimization_barrier(jnp.sum(chances * shift_x, axis=0))
    mean_y = lax.optimization_barrier(jnp.sum(chances * shift_y, axis=0))
    spread = grad_x[None] * shift_x + grad_y[None] * shift_y
    centre = grad_x * mean_x + grad_y * mean_y
    weights = (chances * (spread - centre[None]) / root_depth).astype(jnp.bfloat16)
    query_grad = jnp.zeros((height, columns, channels), jnp.float32)
    band_count = height // HF_DEV
    extended = jnp.zeros((band_count, HF_DEV + 8, columns + 8, channels), jnp.float32)
    for position, (row_step, col_step) in enumerate(shifts):
        weight_wide = weights[position][..., None].astype(jnp.float32)
        query_grad = query_grad + weight_wide * padded[4 + row_step:4 + row_step + height, 4 + col_step:4 + col_step + columns]
        term = (weight_wide * query_wide).reshape(band_count, HF_DEV, columns, channels)
        extended = extended.at[:, 4 + row_step:4 + row_step + HF_DEV, 4 + col_step:4 + col_step + columns].add(term)
    rounded = lax.optimization_barrier(extended[:, :, 4:4 + columns].astype(jnp.bfloat16)).astype(jnp.float32)
    middle = rounded[:, 4:4 + HF_DEV]
    upper = rounded[:, :4]
    lower = rounded[:, 4 + HF_DEV:]
    from_below = jnp.concatenate([upper[1:], jnp.zeros_like(upper[:1])], axis=0)
    from_above = jnp.concatenate([jnp.zeros_like(lower[:1]), lower[:-1]], axis=0)
    summed = middle + jnp.pad(from_below, ((0, 0), (HF_DEV - 4, 0), (0, 0), (0, 0))) + jnp.pad(from_above, ((0, 0), (0, HF_DEV - 4), (0, 0), (0, 0)))
    return (query_grad, summed.reshape(height, columns, channels))

def reference(coarse_features, fine_features, coarse_weight, fine_weight, grad_refined, grad_back):
    frames_count = coarse_features.shape[0]
    positions = jnp.arange(H * W, dtype=jnp.int32)
    coord_x = (positions % W).astype(jnp.float32)
    coord_y = (positions // W).astype(jnp.float32)

    def advance(carry, frame_index):
        carried_q, carried_g, sum_coarse, sum_fine = carry
        following = jnp.minimum(frame_index + 1, frames_count - 1).astype(jnp.int32)
        present = frame_index + 1 < frames_count
        coarse_a = lax.dynamic_index_in_dim(coarse_features, frame_index, 0, keepdims=False).reshape(H * W, C)
        coarse_b = lax.dynamic_index_in_dim(coarse_features, following, 0, keepdims=False).reshape(H * W, C)
        coarse_b = jnp.where(present, coarse_b, jnp.zeros_like(coarse_b))
        fine_a = lax.dynamic_index_in_dim(fine_features, frame_index, 0, keepdims=False)
        fine_b = lax.dynamic_index_in_dim(fine_features, following, 0, keepdims=False)
        fine_b = jnp.where(present, fine_b, jnp.zeros_like(fine_b))
        refined_cot = lax.dynamic_index_in_dim(grad_refined, frame_index, 0, keepdims=False)
        back_cot = lax.dynamic_index_in_dim(grad_back, frame_index, 0, keepdims=False)
        query_a = project(coarse_a, coarse_weight)
        query_b = project(coarse_b, coarse_weight)
        pooled = 4.0 * lax.optimization_barrier(jnp.sum(refined_cot.reshape(2, H, 4, W, 4), axis=(2, 4))).reshape(2, H * W)
        chances_f, top_f, total_f, mean_fx, mean_fy = attend(query_a, query_b, coord_x, coord_y)
        forward_w = weigh(chances_f, pooled[0], pooled[1], mean_fx, mean_fy, coord_x, coord_y, C)
        chances_b, top_b, total_b, mean_bx, mean_by = attend(query_b, query_a, coord_x, coord_y)
        backward_w = weigh(chances_b, back_cot[0], back_cot[1], mean_bx, mean_by, coord_x, coord_y, C)
        dq_first = jnp.dot(forward_w, query_b, preferred_element_type=jnp.float32) + jnp.dot(backward_w.T, query_b, preferred_element_type=jnp.float32)
        dq_second = jnp.dot(backward_w, query_a, preferred_element_type=jnp.float32) + jnp.dot(forward_w.T, query_a, preferred_element_type=jnp.float32)
        second_q = lax.optimization_barrier(dq_second.astype(jnp.bfloat16)).astype(jnp.float32)
        dq_frame = (dq_first + carried_q).astype(jnp.bfloat16)
        coarse_out = jnp.dot(dq_frame, coarse_weight.T, preferred_element_type=jnp.float32).astype(jnp.bfloat16).reshape(H, W, C)
        sum_coarse = sum_coarse + jnp.dot(coarse_a.T, dq_frame, preferred_element_type=jnp.float32)
        local_a = project(fine_a.reshape(HF * WF, FC), fine_weight).reshape(HF, WF, FC)
        local_b = project(fine_b.reshape(HF * WF, FC), fine_weight).reshape(HF, WF, FC)
        refined_grid = refined_cot.reshape(2, HF, WF)
        dg_first, dg_second = fine_pair(local_a, local_b, refined_grid[0], refined_grid[1])
        dg_frame = (dg_first + carried_g).astype(jnp.bfloat16).reshape(HF * WF, FC)
        fine_out = jnp.dot(dg_frame, fine_weight.T, preferred_element_type=jnp.float32).astype(jnp.bfloat16).reshape(HF, WF, FC)
        sum_fine = sum_fine + jnp.dot(fine_a.reshape(HF * WF, FC).T, dg_frame, preferred_element_type=jnp.float32)
        return ((second_q, dg_second, sum_coarse, sum_fine), (coarse_out, fine_out))
    initial = (jnp.zeros((H * W, C), jnp.float32), jnp.zeros((HF, WF, FC), jnp.float32), jnp.zeros((C, C), jnp.float32), jnp.zeros((FC, FC), jnp.float32))
    finished, outputs = lax.scan(advance, initial, jnp.arange(frames_count, dtype=jnp.int32))
    return (outputs[0], outputs[1], finished[2] / frames_count, finished[3] / frames_count)
```

```python
import math

import jax
import jax.numpy as jnp
from jax import lax
from jax.experimental import pallas as pl
from jax.experimental.pallas import tpu as pltpu
from jax.sharding import Mesh, PartitionSpec as P

F32 = jnp.float32
BF16 = jnp.bfloat16
FRAMES = ("z", "yh", "core")
ROWS = ("x", "yl")
PLANE = ("yh", "core", "x", "yl")
ALL = FRAMES + ROWS
N_FRAMES, N_ROWS, N_PLANE, N_Z = 64, 8, 32, 16
COLS = 112
SPAN = 9 * COLS
VMEM = pl.BlockSpec(memory_space=pltpu.VMEM)
SMEM = pl.BlockSpec(memory_space=pltpu.SMEM)


def call(body, outs, scratch=(), n_smem=0, n_in=0, flops=0, nbytes=0):
    return pl.pallas_call(
        body,
        out_shape=outs,
        in_specs=[SMEM] * n_smem + [VMEM] * n_in,
        out_specs=jax.tree.map(lambda _: VMEM, outs),
        scratch_shapes=list(scratch),
        compiler_params=pltpu.CompilerParams(vmem_limit_bytes=40 * 1024 * 1024),
        cost_estimate=pl.CostEstimate(flops=flops, bytes_accessed=nbytes, transcendentals=0),
    )


def shape(*dims, dtype=BF16):
    return jax.ShapeDtypeStruct(dims, dtype)


def mm(a, b):
    return lax.dot_general(a, b, (((1,), (0,)), ((), ())), preferred_element_type=F32)


def mm_nt(a, b):
    return lax.dot_general(a, b, (((1,), (1,)), ((), ())), preferred_element_type=F32)


def mm_tn(a, b):
    return lax.dot_general(a, b, (((0,), (0,)), ((), ())), preferred_element_type=F32)


def split3(value):
    hi = value.astype(BF16)
    rest = value - hi.astype(F32)
    mid = rest.astype(BF16)
    low = (rest - mid.astype(F32)).astype(BF16)
    return hi, mid, low


def iota(dims, axis):
    return lax.broadcasted_iota(jnp.int32, dims, axis)


def prepare_body(coarse, refined, back, out, cots):
    cell = iota((768, 128), 0)
    low = (cell >= 384).astype(jnp.int32)
    cell = cell - 384 * low
    line = (cell >= 96).astype(jnp.int32) + (cell >= 192).astype(jnp.int32) + (cell >= 288).astype(jnp.int32)
    column = lax.shift_right_logical(cell - 96 * line, 2)
    pool = (iota((768, 128), 1) == column + 24 * low).astype(F32).astype(BF16)
    hi, mid, rest = split3(refined[...])
    cots[...] = jnp.zeros_like(cots)
    cots[0:2, 0:128] = 4.0 * (mm(hi, pool) + (mm(mid, pool) + mm(rest, pool)))
    cots[2:4, 0:48] = back[...]
    hi, mid, rest = split3(cots[0:4, :])
    cots[0:4, :] = hi.astype(F32)
    cots[4:8, :] = mid.astype(F32)
    cots[8:12, :] = rest.astype(F32)
    packed = cots[...].astype(BF16)
    for band in range(N_ROWS):
        out[band, 0:48, :] = coarse[...]
        out[band, 48:64, :] = packed


def fine_body(own, middle, above, below, weight, refined, first, mid_out, up_out, down_out, partial,
              queries, keys, key_grad, turned):
    scale = 1.0 / math.sqrt(128.0)
    w = weight[...]
    queries[...] = mm(own[...], w).astype(BF16)
    blank = jnp.zeros((COLS - 96, 128), BF16)
    for row in range(16):
        if row < 4:
            source = above[row * 96 : row * 96 + 96, :]
        elif row < 12:
            source = middle[(row - 4) * 96 : (row - 4) * 96 + 96, :]
        else:
            source = below[(row - 12) * 96 : (row - 12) * 96 + 96, :]
        keys[row * COLS : row * COLS + 96, :] = mm(source, w).astype(BF16)
        keys[row * COLS + 96 : row * COLS + COLS, :] = blank
    key_grad[...] = jnp.zeros_like(key_grad)
    turned[...] = jnp.zeros_like(turned)
    turned[0:2, :] = refined[...]
    cot = jnp.transpose(turned[...], (1, 0))
    lane = iota((1, SPAN), 1).astype(F32)
    line = jnp.floor((lane + 0.5) * (1.0 / COLS))
    column = lane - line * COLS
    step_y = line - 4.0
    step_x = column - iota((96, SPAN), 0).astype(F32)
    step_x = jnp.where(step_x > 50.0, step_x - COLS, step_x)
    inside = jnp.abs(step_x) < 4.5
    for row in range(8):
        q = queries[row * 96 : row * 96 + 96, :]
        k = keys[row * COLS : row * COLS + SPAN, :]
        s = jnp.where(inside, mm_nt(q, k) * scale, -1e30)
        e = jnp.exp(s - jnp.max(s, axis=1, keepdims=True))
        inverse = 1.0 / jnp.sum(e, axis=1, keepdims=True)
        mean_x = jnp.sum(e * step_x, axis=1, keepdims=True) * inverse
        mean_y = jnp.sum(e * step_y, axis=1, keepdims=True) * inverse
        gx = cot[row * 96 : row * 96 + 96, 0:1]
        gy = cot[row * 96 : row * 96 + 96, 1:2]
        factor = inverse * scale
        bend = gx * step_x + gy * step_y - (gx * mean_x + gy * mean_y)
        weights = (e * bend * factor).astype(BF16)
        first[row * 96 : row * 96 + 96, :] = mm(weights, k)
        key_grad[row * COLS : row * COLS + SPAN, :] += mm_tn(weights, q)
    for row in range(16):
        rounded = key_grad[row * COLS : row * COLS + 96, :].astype(BF16)
        if row < 4:
            up_out[row * 96 : row * 96 + 96, :] = rounded
        elif row < 12:
            mid_out[(row - 4) * 96 : (row - 4) * 96 + 96, :] = rounded
        else:
            down_out[(row - 12) * 96 : (row - 12) * 96 + 96, :] = rounded
    hi = first[...].astype(BF16)
    low = (first[...] - hi.astype(F32)).astype(BF16)
    total = mm_tn(own[...], hi) + mm_tn(own[...], low)
    total = total + mm_tn(middle[...], mid_out[...])
    partial[...] = total + mm_tn(above[...], up_out[...]) + mm_tn(below[...], down_out[...])


def coarse_body(position, here, there, weight, fine_partial, first, second, send,
                forward, backward, both, packed):
    band = position[0]
    w = weight[...]
    qa = mm(here[:, 0:48, :].reshape(384, 256), w).astype(BF16)
    qb = mm(there[:, 0:48, :].reshape(384, 256), w).astype(BF16)
    flat = jnp.zeros((16, 384), F32)
    upright = jnp.zeros((384, 16), F32)
    for source in range(N_ROWS):
        cots = here[source, 48:64, 0:128]
        place = (iota((128, 384), 1) - iota((128, 384), 0) == 48 * source).astype(F32).astype(BF16)
        turned = (iota((384, 128), 0) - iota((384, 128), 1) == 48 * source).astype(F32).astype(BF16)
        flat = flat + mm(cots, place)
        upright = upright + mm_nt(turned, cots)
    cf_x = upright[:, 0:1] + (upright[:, 4:5] + upright[:, 8:9])
    cf_y = upright[:, 1:2] + (upright[:, 5:6] + upright[:, 9:10])
    cb_x = flat[2:3, :] + (flat[6:7, :] + flat[10:11, :])
    cb_y = flat[3:4, :] + (flat[7:8, :] + flat[11:12, :])
    lane = iota((1, 384), 1).astype(F32)
    lane_y = jnp.floor((lane + 0.5) * (1.0 / 24.0))
    lane_x = lane - 24.0 * lane_y
    line = iota((384, 1), 0).astype(F32)
    line_y = jnp.floor((line + 0.5) * (1.0 / 24.0))
    line_x = line - 24.0 * line_y
    s = mm_nt(qa, qb) * (1.0 / 16.0)
    e = jnp.exp(s - jnp.max(s, axis=1, keepdims=True))
    inverse = 1.0 / jnp.sum(e, axis=1, keepdims=True)
    mean_x = jnp.sum(e * lane_x, axis=1, keepdims=True) * inverse
    mean_y = jnp.sum(e * lane_y, axis=1, keepdims=True) * inverse
    bend = cf_x * lane_x + cf_y * lane_y - (cf_x * mean_x + cf_y * mean_y)
    forward_w = (e * bend * (inverse * (1.0 / 16.0))).astype(BF16)
    forward[...] = forward_w
    e = jnp.exp(s - jnp.max(s, axis=0, keepdims=True))
    inverse = 1.0 / jnp.sum(e, axis=0, keepdims=True)
    mean_x = jnp.sum(e * line_x, axis=0, keepdims=True) * inverse
    mean_y = jnp.sum(e * line_y, axis=0, keepdims=True) * inverse
    bend = cb_x * line_x + cb_y * line_y - (cb_x * mean_x + cb_y * mean_y)
    backward_w = (e * bend * (inverse * (1.0 / 16.0))).astype(BF16)
    backward[...] = backward_w
    both[...] = mm_tn(forward_w, qa) + mm_tn(backward_w, qa)
    mine = pl.ds(pl.multiple_of(band * 48, 16), 48)
    own_first = mm(forward[mine, :], qb) + mm(backward[mine, :], qb)
    own_second = both[mine, :].astype(BF16)
    first[...] = own_first
    second[...] = own_second
    hi = own_first.astype(BF16)
    low = (own_first - hi.astype(F32)).astype(BF16)
    f_here = here[band, 0:48, :]
    total = mm_tn(f_here, hi) + mm_tn(f_here, low) + mm_tn(there[band, 0:48, :], own_second)
    packed[:, 0:8, :] = total[:, 0:128].reshape(N_PLANE, 8, 128)
    packed[:, 8:16, :] = total[:, 128:256].reshape(N_PLANE, 8, 128)
    for chunk in range(N_PLANE):
        packed[chunk, 16:20, :] = fine_partial[4 * chunk : 4 * chunk + 4, :]
    send[...] = packed[...][:, 0:20, :].astype(BF16)


def sum_body(parts, out):
    total = parts[0].astype(F32)
    for source in range(1, parts.shape[0]):
        total = total + parts[source].astype(F32)
    rounded = total.astype(BF16)
    for target in range(out.shape[0]):
        out[target] = rounded


def unpack_body(parts, coarse, fine):
    values = parts[...].astype(F32) * (1.0 / N_FRAMES)
    coarse[:, 0:128] = values[:, 0:8, :].reshape(256, 128)
    coarse[:, 128:256] = values[:, 8:16, :].reshape(256, 128)
    for chunk in range(N_PLANE):
        fine[4 * chunk : 4 * chunk + 4, :] = values[chunk, 16:20, :]


def finish_body(first, middle, from_above, from_below, weight, coarse_first, coarse_second, coarse_weight,
                fine_out, coarse_out):
    total = first[...] + middle[...].astype(F32)
    w = weight[...]
    top = (total[0:384, :] + from_above[...].astype(F32)).astype(BF16)
    bottom = (total[384:768, :] + from_below[...].astype(F32)).astype(BF16)
    fine_out[0:384, :] = mm_nt(top, w).astype(BF16)
    fine_out[384:768, :] = mm_nt(bottom, w).astype(BF16)
    dq = (coarse_first[...] + coarse_second[...].astype(F32)).astype(BF16)
    coarse_out[...] = mm_nt(dq, coarse_weight[...]).astype(BF16)


def shifted(value, frames, rows):
    pairs = [
        (f * N_ROWS + r, (f + frames) * N_ROWS + r + rows)
        for f in range(max(0, -frames), min(N_FRAMES, N_FRAMES - frames))
        for r in range(max(0, -rows), min(N_ROWS, N_ROWS - rows))
    ]
    return lax.ppermute(value, ALL, pairs)


def local(coarse_features, fine_features, coarse_weight, fine_weight, grad_refined, grad_back):
    coarse_own = coarse_features.reshape(48, 256)
    fine_own = fine_features.reshape(768, 128)
    refined = grad_refined.reshape(2, 768)
    band = lax.axis_index(ROWS).astype(jnp.int32).reshape(1)
    middle = shifted(fine_own, -1, 0)
    above = shifted(fine_own[384:768], -1, 1)
    below = shifted(fine_own[0:384], -1, -1)
    outgoing = call(prepare_body, shape(N_ROWS, 64, 256), [pltpu.VMEM((16, 256), F32)], n_in=3,
                    flops=10**8, nbytes=10**6)(coarse_own, refined, grad_back.reshape(2, 48))
    here = lax.all_to_all(outgoing, ROWS, 0, 0, tiled=True)
    there = shifted(here, -1, 0)
    first, mid_out, up_out, down_out, fine_partial = call(
        fine_body,
        (shape(768, 128, dtype=F32), shape(768, 128), shape(384, 128), shape(384, 128), shape(128, 128, dtype=F32)),
        [
            pltpu.VMEM((768, 128), BF16),
            pltpu.VMEM((16 * COLS, 128), BF16),
            pltpu.VMEM((16 * COLS, 128), F32),
            pltpu.VMEM((8, 768), F32),
        ],
        n_in=6, flops=10**9, nbytes=4 * 10**6,
    )(fine_own, middle, above, below, fine_weight, refined)
    back_up = shifted(up_out, 1, -1)
    back_down = shifted(down_out, 1, 1)
    back_mid = shifted(mid_out, 1, 0)
    coarse_first, coarse_second, send = call(
        coarse_body,
        (shape(48, 256, dtype=F32), shape(48, 256), shape(N_PLANE, 20, 128)),
        [
            pltpu.VMEM((384, 384), BF16),
            pltpu.VMEM((384, 384), BF16),
            pltpu.VMEM((384, 256), F32),
            pltpu.VMEM((N_PLANE, 24, 128), F32),
        ],
        n_smem=1, n_in=4, flops=10**9, nbytes=2 * 10**6,
    )(band, here, there, coarse_weight, fine_partial)
    back_coarse = shifted(coarse_second, 1, 0)
    parts = lax.all_to_all(send, PLANE, 0, 0, tiled=True)
    copies = call(sum_body, shape(N_Z, 20, 128), n_in=1, nbytes=10**6)(parts)
    parts = lax.all_to_all(copies, "z", 0, 0, tiled=True)
    copies = call(sum_body, shape(N_PLANE, 20, 128), n_in=1, nbytes=10**6)(parts)
    parts = lax.all_to_all(copies, PLANE, 0, 0, tiled=True)
    coarse_total, fine_total = call(
        unpack_body, (shape(256, 256, dtype=F32), shape(128, 128, dtype=F32)), n_in=1, nbytes=10**6
    )(parts)
    fine_grad, coarse_grad = call(
        finish_body, (shape(768, 128), shape(48, 256)), n_in=8, flops=10**8, nbytes=10**6
    )(first, back_mid, back_down, back_up, fine_weight, coarse_first, back_coarse, coarse_weight)
    return (
        coarse_grad.reshape(coarse_features.shape),
        fine_grad.reshape(fine_features.shape),
        coarse_total,
        fine_total,
    )


def solution(mesh):
    fine_mesh = Mesh(mesh.devices.reshape(16, 2, 2, 4, 2), ALL)
    in_specs = (
        P(FRAMES, ROWS, None, None),
        P(FRAMES, ROWS, None, None),
        P(),
        P(),
        P(FRAMES, None, ROWS),
        P(FRAMES, None, ROWS),
    )
    out_specs = (P(FRAMES, ROWS, None, None), P(FRAMES, ROWS, None, None), P(), P())
    return jax.shard_map(local, mesh=fine_mesh, in_specs=in_specs, out_specs=out_specs, check_vma=False)
```

```python
import math

import jax
import jax.numpy as jnp
from jax import lax
from jax.experimental import pallas as pl
from jax.experimental.pallas import tpu as pltpu
from jax.sharding import Mesh, PartitionSpec as P

F32 = jnp.float32
BF16 = jnp.bfloat16
FRAMES = ("z", "yh", "core")
ROWS = ("x", "yl")
PLANE = ("yh", "core", "x", "yl")
ALL = FRAMES + ROWS
N_FRAMES, N_ROWS, N_PLANE, N_Z = 64, 8, 32, 16
VMEM = pl.BlockSpec(memory_space=pltpu.VMEM)
HBM = pl.BlockSpec(memory_space=pltpu.HBM)
SMEM = pl.BlockSpec(memory_space=pltpu.SMEM)


def call(body, outs, scratch=(), n_smem=0, n_in=0, flops=0, nbytes=0, kind=VMEM):
    return pl.pallas_call(
        body,
        out_shape=outs,
        in_specs=[SMEM] * n_smem + [kind] * n_in,
        out_specs=jax.tree.map(lambda _: VMEM, outs),
        scratch_shapes=list(scratch),
        compiler_params=pltpu.CompilerParams(vmem_limit_bytes=40 * 1024 * 1024),
        cost_estimate=pl.CostEstimate(flops=flops, bytes_accessed=nbytes, transcendentals=0),
    )


def shape(*dims, dtype=BF16):
    return jax.ShapeDtypeStruct(dims, dtype)


def mm(a, b):
    return lax.dot_general(a, b, (((1,), (0,)), ((), ())), preferred_element_type=F32)


def mm_nt(a, b):
    return lax.dot_general(a, b, (((1,), (1,)), ((), ())), preferred_element_type=F32)


def mm_tn(a, b):
    return lax.dot_general(a, b, (((0,), (0,)), ((), ())), preferred_element_type=F32)


def split3(value):
    hi = value.astype(BF16)
    rest = value - hi.astype(F32)
    mid = rest.astype(BF16)
    low = (rest - mid.astype(F32)).astype(BF16)
    return hi, mid, low


def iota(dims, axis):
    return lax.broadcasted_iota(jnp.int32, dims, axis)


def prepare_body(coarse_hbm, refined_hbm, back_hbm, out, cots, refined, back, sems):
    copies = [
        pltpu.make_async_copy(refined_hbm, refined, sems.at[N_ROWS]),
        pltpu.make_async_copy(back_hbm, back, sems.at[N_ROWS + 1]),
    ]
    for band in range(N_ROWS):
        copies.append(pltpu.make_async_copy(coarse_hbm, out.at[band, pl.ds(0, 48), :], sems.at[band]))
    for copy in copies:
        copy.start()
    cell = iota((768, 128), 0)
    low = (cell >= 384).astype(jnp.int32)
    cell = cell - 384 * low
    line = (cell >= 96).astype(jnp.int32) + (cell >= 192).astype(jnp.int32) + (cell >= 288).astype(jnp.int32)
    column = lax.shift_right_logical(cell - 96 * line, 2)
    pool = (iota((768, 128), 1) == column + 24 * low).astype(F32).astype(BF16)
    cots[...] = jnp.zeros_like(cots)
    copies[0].wait()
    copies[1].wait()
    hi, mid, rest = split3(refined[...])
    cots[0:2, 0:128] = 4.0 * (mm(hi, pool) + (mm(mid, pool) + mm(rest, pool)))
    cots[2:4, 0:48] = back[...]
    hi, mid, rest = split3(cots[0:4, :])
    cots[0:4, :] = hi.astype(F32)
    cots[4:8, :] = mid.astype(F32)
    cots[8:12, :] = rest.astype(F32)
    packed = cots[...].astype(BF16)
    for band in range(N_ROWS):
        out[band, 48:64, :] = packed
    for copy in copies[2:]:
        copy.wait()


def fine_body(own, middle, above, below, weight, refined, first, mid_out, up_out, down_out, partial,
              queries, keys, key_grad, turned, window):
    scale = 1.0 / math.sqrt(128.0)
    w = weight[...]
    queries[...] = mm(own[...], w).astype(BF16).reshape(8, 96, 128)
    keys[:, 0:16, :] = jnp.zeros((16, 16, 128), BF16)
    keys[:, 112:128, :] = jnp.zeros((16, 16, 128), BF16)
    keys[0:4, 16:112, :] = mm(above[...], w).astype(BF16).reshape(4, 96, 128)
    keys[4:12, 16:112, :] = mm(middle[...], w).astype(BF16).reshape(8, 96, 128)
    keys[12:16, 16:112, :] = mm(below[...], w).astype(BF16).reshape(4, 96, 128)
    key_grad[...] = jnp.zeros_like(key_grad)
    turned[...] = jnp.zeros_like(turned)
    turned[0:2, :] = refined[...]
    upright = jnp.transpose(turned[...], (1, 0))
    lane = iota((1, 128), 1)
    query_x = jnp.bitwise_and(lane, 31).astype(F32)
    query_y = lax.shift_right_logical(lane, 5).astype(F32)
    key_x = iota((64, 128), 0).astype(F32) - 16.0
    near_x = jnp.where(jnp.abs(key_x - query_x) < 4.5, 0.0, -1e30)
    for line in range(12):
        near_y = jnp.where(jnp.abs(line - 4.0 - query_y) < 4.5, 0.0, -1e30)
        window[line] = jnp.minimum(near_x, near_y)
    for part in range(2):
        for column in range(3):
            q = queries[4 * part : 4 * part + 4, 32 * column : 32 * column + 32, :].reshape(128, 128)
            k = keys[4 * part : 4 * part + 12, 32 * column : 32 * column + 64, :].reshape(768, 128)
            pieces = [(4 * part + line) * 96 + 32 * column for line in range(4)]
            cot = jnp.transpose(jnp.concatenate([upright[at : at + 32, :] for at in pieces], axis=0), (1, 0))
            gx, gy = cot[0:1, :], cot[1:2, :]
            s = mm_nt(k, q).reshape(12, 64, 128) * (scale * math.log2(math.e)) + window[...]
            top = jnp.max(jnp.max(s, axis=0), axis=0, keepdims=True)
            e = jnp.exp2(s - top)
            by_x = jnp.sum(e, axis=0)
            inverse = 1.0 / jnp.sum(by_x, axis=0, keepdims=True)
            mean_x = jnp.sum(by_x * key_x, axis=0, keepdims=True) * inverse
            mean_y = jnp.zeros((1, 128), F32)
            for line in range(12):
                mean_y = mean_y + (line - 4.0) * jnp.sum(e[line], axis=0, keepdims=True)
            mean_y = mean_y * inverse
            factor = inverse * scale
            gx, gy = gx * factor, gy * factor
            bend_x = gx * (key_x - mean_x)
            weights = jnp.concatenate(
                [(e[line] * (bend_x + gy * ((line - 4.0) - mean_y))).astype(BF16) for line in range(12)], axis=0
            )
            first[4 * part : 4 * part + 4, 32 * column : 32 * column + 32, :] = mm_tn(weights, k).reshape(4, 32, 128)
            key_grad[4 * part : 4 * part + 12, 32 * column : 32 * column + 64, :] += mm(weights, q).reshape(12, 64, 128)
    up_out[...] = key_grad[0:4, 16:112, :].astype(BF16).reshape(384, 128)
    mid_out[...] = key_grad[4:12, 16:112, :].astype(BF16).reshape(768, 128)
    down_out[...] = key_grad[12:16, 16:112, :].astype(BF16).reshape(384, 128)
    exact = first[...].reshape(768, 128)
    hi = exact.astype(BF16)
    low = (exact - hi.astype(F32)).astype(BF16)
    total = mm_tn(own[...], hi) + mm_tn(own[...], low)
    total = total + mm_tn(middle[...], mid_out[...])
    partial[...] = total + mm_tn(above[...], up_out[...]) + mm_tn(below[...], down_out[...])


def coarse_body(position, here, there, weight, fine_partial, fine_middle, first, joined, send,
                forward, backward, both, packed):
    band = position[0]
    w = weight[...]
    qa = mm(here[:, 0:48, :].reshape(384, 256), w).astype(BF16)
    qb = mm(there[:, 0:48, :].reshape(384, 256), w).astype(BF16)
    flat = jnp.zeros((16, 384), F32)
    upright = jnp.zeros((384, 16), F32)
    for source in range(N_ROWS):
        cots = here[source, 48:64, 0:128]
        place = (iota((128, 384), 1) - iota((128, 384), 0) == 48 * source).astype(F32).astype(BF16)
        turned = (iota((384, 128), 0) - iota((384, 128), 1) == 48 * source).astype(F32).astype(BF16)
        flat = flat + mm(cots, place)
        upright = upright + mm_nt(turned, cots)
    cf_x = upright[:, 0:1] + (upright[:, 4:5] + upright[:, 8:9])
    cf_y = upright[:, 1:2] + (upright[:, 5:6] + upright[:, 9:10])
    cb_x = flat[2:3, :] + (flat[6:7, :] + flat[10:11, :])
    cb_y = flat[3:4, :] + (flat[7:8, :] + flat[11:12, :])
    lane = iota((1, 384), 1).astype(F32)
    lane_y = jnp.floor((lane + 0.5) * (1.0 / 24.0))
    lane_x = lane - 24.0 * lane_y
    line = iota((384, 1), 0).astype(F32)
    line_y = jnp.floor((line + 0.5) * (1.0 / 24.0))
    line_x = line - 24.0 * line_y
    s = mm_nt(qa, qb) * (1.0 / 16.0)
    e = jnp.exp(s - jnp.max(s, axis=1, keepdims=True))
    inverse = 1.0 / jnp.sum(e, axis=1, keepdims=True)
    mean_x = jnp.sum(e * lane_x, axis=1, keepdims=True) * inverse
    mean_y = jnp.sum(e * lane_y, axis=1, keepdims=True) * inverse
    bend = cf_x * lane_x + cf_y * lane_y - (cf_x * mean_x + cf_y * mean_y)
    forward_w = (e * bend * (inverse * (1.0 / 16.0))).astype(BF16)
    forward[...] = forward_w
    e = jnp.exp(s - jnp.max(s, axis=0, keepdims=True))
    inverse = 1.0 / jnp.sum(e, axis=0, keepdims=True)
    mean_x = jnp.sum(e * line_x, axis=0, keepdims=True) * inverse
    mean_y = jnp.sum(e * line_y, axis=0, keepdims=True) * inverse
    bend = cb_x * line_x + cb_y * line_y - (cb_x * mean_x + cb_y * mean_y)
    backward_w = (e * bend * (inverse * (1.0 / 16.0))).astype(BF16)
    backward[...] = backward_w
    both[...] = mm_tn(forward_w, qa) + mm_tn(backward_w, qa)
    mine = pl.ds(pl.multiple_of(band * 48, 16), 48)
    own_first = mm(forward[mine, :], qb) + mm(backward[mine, :], qb)
    own_second = both[mine, :].astype(BF16)
    first[...] = own_first
    joined[0:768, :] = fine_middle[...]
    joined[768:816, :] = own_second[:, 0:128]
    joined[816:864, :] = own_second[:, 128:256]
    hi = own_first.astype(BF16)
    low = (own_first - hi.astype(F32)).astype(BF16)
    f_here = here[band, 0:48, :]
    total = mm_tn(f_here, hi) + mm_tn(f_here, low) + mm_tn(there[band, 0:48, :], own_second)
    packed[:, 0:8, :] = total[:, 0:128].reshape(N_PLANE, 8, 128)
    packed[:, 8:16, :] = total[:, 128:256].reshape(N_PLANE, 8, 128)
    for chunk in range(N_PLANE):
        packed[chunk, 16:20, :] = fine_partial[4 * chunk : 4 * chunk + 4, :]
    send[...] = packed[...][:, 0:20, :].astype(BF16)


def sum_body(parts, out):
    total = parts[0].astype(F32)
    for source in range(1, parts.shape[0]):
        total = total + parts[source].astype(F32)
    rounded = total.astype(BF16)
    for target in range(out.shape[0]):
        out[target] = rounded


def unpack_body(parts, coarse, fine):
    values = parts[...].astype(F32) * (1.0 / N_FRAMES)
    coarse[:, 0:128] = values[:, 0:8, :].reshape(256, 128)
    coarse[:, 128:256] = values[:, 8:16, :].reshape(256, 128)
    for chunk in range(N_PLANE):
        fine[4 * chunk : 4 * chunk + 4, :] = values[chunk, 16:20, :]


def finish_body(first, joined, from_above, from_below, weight, coarse_first, coarse_weight, fine_out, coarse_out):
    total = first[...] + joined[0:768, :].astype(F32)
    w = weight[...]
    top = (total[0:384, :] + from_above[...].astype(F32)).astype(BF16)
    bottom = (total[384:768, :] + from_below[...].astype(F32)).astype(BF16)
    fine_out[0:384, :] = mm_nt(top, w).astype(BF16)
    fine_out[384:768, :] = mm_nt(bottom, w).astype(BF16)
    w = coarse_weight[...]
    left = (coarse_first[:, 0:128] + joined[768:816, :].astype(F32)).astype(BF16)
    right = (coarse_first[:, 128:256] + joined[816:864, :].astype(F32)).astype(BF16)
    coarse_out[...] = (mm_nt(left, w[:, 0:128]) + mm_nt(right, w[:, 128:256])).astype(BF16)


def shifted(value, frames, rows):
    pairs = [
        (f * N_ROWS + r, (f + frames) * N_ROWS + r + rows)
        for f in range(max(0, -frames), min(N_FRAMES, N_FRAMES - frames))
        for r in range(max(0, -rows), min(N_ROWS, N_ROWS - rows))
    ]
    return lax.ppermute(value, ALL, pairs)


def local(coarse_features, fine_features, coarse_weight, fine_weight, grad_refined, grad_back):
    coarse_own = coarse_features.reshape(48, 256)
    fine_own = fine_features.reshape(768, 128)
    refined = grad_refined.reshape(2, 768)
    band = lax.axis_index(ROWS).astype(jnp.int32).reshape(1)
    middle = shifted(fine_own, -1, 0)
    above = shifted(fine_own[384:768], -1, 1)
    below = shifted(fine_own[0:384], -1, -1)
    outgoing = call(
        prepare_body,
        shape(N_ROWS, 64, 256),
        [
            pltpu.VMEM((16, 256), F32),
            pltpu.VMEM((2, 768), F32),
            pltpu.VMEM((2, 48), F32),
            pltpu.SemaphoreType.DMA((N_ROWS + 2,)),
        ],
        n_in=3, flops=10**9, nbytes=10**6, kind=HBM,
    )(coarse_own, refined, grad_back.reshape(2, 48))
    here = lax.all_to_all(outgoing, ROWS, 0, 0, tiled=True)
    there = shifted(here, -1, 0)
    first, mid_out, up_out, down_out, fine_partial = call(
        fine_body,
        (shape(8, 96, 128, dtype=F32), shape(768, 128), shape(384, 128), shape(384, 128), shape(128, 128, dtype=F32)),
        [
            pltpu.VMEM((8, 96, 128), BF16),
            pltpu.VMEM((16, 128, 128), BF16),
            pltpu.VMEM((16, 128, 128), F32),
            pltpu.VMEM((8, 768), F32),
            pltpu.VMEM((12, 64, 128), F32),
        ],
        n_in=6, flops=20 * 10**9, nbytes=4 * 10**6,
    )(fine_own, middle, above, below, fine_weight, refined)
    back_up = shifted(up_out, 1, -1)
    back_down = shifted(down_out, 1, 1)
    coarse_first, joined, send = call(
        coarse_body,
        (shape(48, 256, dtype=F32), shape(864, 128), shape(N_PLANE, 20, 128)),
        [
            pltpu.VMEM((384, 384), BF16),
            pltpu.VMEM((384, 384), BF16),
            pltpu.VMEM((384, 256), F32),
            pltpu.VMEM((N_PLANE, 24, 128), F32),
        ],
        n_smem=1, n_in=5, flops=3 * 10**9, nbytes=2 * 10**6,
    )(band, here, there, coarse_weight, fine_partial, mid_out)
    back_joined = shifted(joined, 1, 0)
    parts = lax.all_to_all(send, PLANE, 0, 0, tiled=True)
    parts, back_up, back_down = lax.optimization_barrier((parts, back_up, back_down))
    copies = call(sum_body, shape(N_Z, 20, 128), n_in=1, nbytes=10**6)(parts)
    parts = lax.all_to_all(copies, "z", 0, 0, tiled=True)
    parts, back_joined = lax.optimization_barrier((parts, back_joined))
    copies = call(sum_body, shape(N_PLANE, 20, 128), n_in=1, nbytes=10**6)(parts)
    parts = lax.all_to_all(copies, PLANE, 0, 0, tiled=True)
    coarse_total, fine_total = call(
        unpack_body, (shape(256, 256, dtype=F32), shape(128, 128, dtype=F32)), n_in=1, nbytes=10**6
    )(parts)
    fine_grad, coarse_grad = call(
        finish_body, (shape(768, 128), shape(48, 256)), n_in=7, flops=10**8, nbytes=10**6
    )(first.reshape(768, 128), back_joined, back_down, back_up, fine_weight, coarse_first, coarse_weight)
    return (
        coarse_grad.reshape(coarse_features.shape),
        fine_grad.reshape(fine_features.shape),
        coarse_total,
        fine_total,
    )


def solution(mesh):
    fine_mesh = Mesh(mesh.devices.reshape(16, 2, 2, 4, 2), ALL)
    in_specs = (
        P(FRAMES, ROWS, None, None),
        P(FRAMES, ROWS, None, None),
        P(),
        P(),
        P(FRAMES, None, ROWS),
        P(FRAMES, None, ROWS),
    )
    out_specs = (P(FRAMES, ROWS, None, None), P(FRAMES, ROWS, None, None), P(), P())
    return jax.shard_map(local, mesh=fine_mesh, in_specs=in_specs, out_specs=out_specs, check_vma=False)
```

```python
import math

import jax
import jax.numpy as jnp
from jax import lax
from jax.experimental import pallas as pl
from jax.experimental.pallas import tpu as pltpu
from jax.sharding import Mesh, PartitionSpec as P

F32 = jnp.float32
BF16 = jnp.bfloat16
FRAMES = ("z", "yh", "core")
ROWS = ("x", "yl")
PLANE = ("yh", "core", "x", "yl")
ALL = FRAMES + ROWS
N_FRAMES, N_ROWS, N_PLANE, N_Z = 64, 8, 32, 16
VMEM = pl.BlockSpec(memory_space=pltpu.VMEM)
HBM = pl.BlockSpec(memory_space=pltpu.HBM)
SMEM = pl.BlockSpec(memory_space=pltpu.SMEM)


def call(body, outs, scratch=(), n_smem=0, n_in=0, flops=0, nbytes=0, kind=VMEM, room=40):
    return pl.pallas_call(
        body,
        out_shape=outs,
        in_specs=[SMEM] * n_smem + [kind] * n_in,
        out_specs=jax.tree.map(lambda _: VMEM, outs),
        scratch_shapes=list(scratch),
        compiler_params=pltpu.CompilerParams(vmem_limit_bytes=room * 1024 * 1024),
        cost_estimate=pl.CostEstimate(flops=flops, bytes_accessed=nbytes, transcendentals=0),
    )


def shape(*dims, dtype=BF16):
    return jax.ShapeDtypeStruct(dims, dtype)


def mm(a, b):
    return lax.dot_general(a, b, (((1,), (0,)), ((), ())), preferred_element_type=F32)


def mm_nt(a, b):
    return lax.dot_general(a, b, (((1,), (1,)), ((), ())), preferred_element_type=F32)


def mm_tn(a, b):
    return lax.dot_general(a, b, (((0,), (0,)), ((), ())), preferred_element_type=F32)


def split3(value):
    hi = value.astype(BF16)
    rest = value - hi.astype(F32)
    mid = rest.astype(BF16)
    low = (rest - mid.astype(F32)).astype(BF16)
    return hi, mid, low


def iota(dims, axis):
    return lax.broadcasted_iota(jnp.int32, dims, axis)


def prepare_body(coarse_hbm, refined_hbm, back_hbm, out, cots, refined, back, sems):
    copies = [
        pltpu.make_async_copy(refined_hbm, refined, sems.at[N_ROWS]),
        pltpu.make_async_copy(back_hbm, back, sems.at[N_ROWS + 1]),
    ]
    for band in range(N_ROWS):
        copies.append(pltpu.make_async_copy(coarse_hbm, out.at[band, pl.ds(0, 48), :], sems.at[band]))
    for copy in copies:
        copy.start()
    cell = iota((768, 128), 0)
    low = (cell >= 384).astype(jnp.int32)
    cell = cell - 384 * low
    line = (cell >= 96).astype(jnp.int32) + (cell >= 192).astype(jnp.int32) + (cell >= 288).astype(jnp.int32)
    column = lax.shift_right_logical(cell - 96 * line, 2)
    pool = (iota((768, 128), 1) == column + 24 * low).astype(F32).astype(BF16)
    cots[...] = jnp.zeros_like(cots)
    copies[0].wait()
    copies[1].wait()
    hi, mid, rest = split3(refined[...])
    cots[0:2, 0:128] = 4.0 * (mm(hi, pool) + (mm(mid, pool) + mm(rest, pool)))
    cots[2:4, 0:48] = back[...]
    hi, mid, rest = split3(cots[0:4, :])
    cots[0:4, :] = hi.astype(F32)
    cots[4:8, :] = mid.astype(F32)
    cots[8:12, :] = rest.astype(F32)
    packed = cots[...].astype(BF16)
    for band in range(N_ROWS):
        out[band, 48:64, :] = packed
    for copy in copies[2:]:
        copy.wait()


def fine_body(own, middle, above, below, weight, refined, first, mid_out, up_out, down_out, partial,
              queries, keys, key_grad, turned, window):
    scale = 1.0 / math.sqrt(128.0)
    w = weight[...]
    queries[...] = mm(own[...], w).astype(BF16).reshape(8, 96, 128)
    keys[:, 0:16, :] = jnp.zeros((16, 16, 128), BF16)
    keys[:, 112:128, :] = jnp.zeros((16, 16, 128), BF16)
    keys[0:4, 16:112, :] = mm(above[...], w).astype(BF16).reshape(4, 96, 128)
    keys[4:12, 16:112, :] = mm(middle[...], w).astype(BF16).reshape(8, 96, 128)
    keys[12:16, 16:112, :] = mm(below[...], w).astype(BF16).reshape(4, 96, 128)
    key_grad[...] = jnp.zeros_like(key_grad)
    turned[...] = jnp.zeros_like(turned)
    turned[0:2, :] = refined[...]
    upright = jnp.transpose(turned[...], (1, 0))
    lane = iota((1, 128), 1)
    query_x = jnp.bitwise_and(lane, 31).astype(F32)
    query_y = lax.shift_right_logical(lane, 5).astype(F32)
    key_x = iota((64, 128), 0).astype(F32) - 16.0
    near_x = jnp.where(jnp.abs(key_x - query_x) < 4.5, 0.0, -1e30)
    for line in range(12):
        near_y = jnp.where(jnp.abs(line - 4.0 - query_y) < 4.5, 0.0, -1e30)
        window[line] = jnp.minimum(near_x, near_y)
    for part in range(2):
        for column in range(3):
            q = queries[4 * part : 4 * part + 4, 32 * column : 32 * column + 32, :].reshape(128, 128)
            k = keys[4 * part : 4 * part + 12, 32 * column : 32 * column + 64, :].reshape(768, 128)
            pieces = [(4 * part + line) * 96 + 32 * column for line in range(4)]
            cot = jnp.transpose(jnp.concatenate([upright[at : at + 32, :] for at in pieces], axis=0), (1, 0))
            gx, gy = cot[0:1, :], cot[1:2, :]
            s = mm_nt(k, q).reshape(12, 64, 128) * (scale * math.log2(math.e)) + window[...]
            top = jnp.max(jnp.max(s, axis=0), axis=0, keepdims=True)
            e = jnp.exp2(s - top)
            by_x = jnp.sum(e, axis=0)
            inverse = 1.0 / jnp.sum(by_x, axis=0, keepdims=True)
            mean_x = jnp.sum(by_x * key_x, axis=0, keepdims=True) * inverse
            mean_y = jnp.zeros((1, 128), F32)
            for line in range(12):
                mean_y = mean_y + (line - 4.0) * jnp.sum(e[line], axis=0, keepdims=True)
            mean_y = mean_y * inverse
            factor = inverse * scale
            gx, gy = gx * factor, gy * factor
            bend_x = gx * (key_x - mean_x)
            weights = jnp.concatenate(
                [(e[line] * (bend_x + gy * ((line - 4.0) - mean_y))).astype(BF16) for line in range(12)], axis=0
            )
            first[4 * part : 4 * part + 4, 32 * column : 32 * column + 32, :] = mm_tn(weights, k).reshape(4, 32, 128)
            key_grad[4 * part : 4 * part + 12, 32 * column : 32 * column + 64, :] += mm(weights, q).reshape(12, 64, 128)
    up_out[...] = key_grad[0:4, 16:112, :].astype(BF16).reshape(384, 128)
    mid_out[...] = key_grad[4:12, 16:112, :].astype(BF16).reshape(768, 128)
    down_out[...] = key_grad[12:16, 16:112, :].astype(BF16).reshape(384, 128)
    exact = first[...].reshape(768, 128)
    hi = exact.astype(BF16)
    low = (exact - hi.astype(F32)).astype(BF16)
    total = mm_tn(own[...], hi) + mm_tn(own[...], low)
    total = total + mm_tn(middle[...], mid_out[...])
    partial[...] = total + mm_tn(above[...], up_out[...]) + mm_tn(below[...], down_out[...])


def match(scores, cot_x, cot_y):
    s = scores * (math.log2(math.e) / 16.0)
    e = jnp.exp2(s - jnp.max(s, axis=0, keepdims=True)).reshape(16, 24, 384)
    by_x = jnp.sum(e, axis=0)
    inverse = 1.0 / jnp.sum(by_x, axis=0, keepdims=True)
    key_x = iota((24, 384), 0).astype(F32)
    mean_x = jnp.sum(by_x * key_x, axis=0, keepdims=True) * inverse
    mean_y = jnp.zeros((1, 384), F32)
    for line in range(1, 16):
        mean_y = mean_y + float(line) * jnp.sum(e[line], axis=0, keepdims=True)
    mean_y = mean_y * inverse
    factor = inverse * (1.0 / 16.0)
    cot_x, cot_y = cot_x * factor, cot_y * factor
    bend_x = cot_x * (key_x - mean_x)
    lines = [e[line] * (bend_x + cot_y * (float(line) - mean_y)) for line in range(16)]
    return jnp.concatenate(lines, axis=0).astype(BF16)


def coarse_body(position, here, there, weight, fine_partial, fine_middle, first, joined, send,
                sums_first, sums_second, packed):
    band = position[0]
    w = weight[...]
    qa = mm(here[:, 0:48, :].reshape(384, 256), w).astype(BF16)
    qb = mm(there[:, 0:48, :].reshape(384, 256), w).astype(BF16)
    flat = jnp.zeros((16, 384), F32)
    ahead = iota((128, 384), 1) - iota((128, 384), 0)
    for source in range(N_ROWS):
        place = (ahead == 48 * source).astype(F32).astype(BF16)
        flat = flat + mm(here[source, 48:64, 0:128], place)
    cots = flat[0:4, :] + (flat[4:8, :] + flat[8:12, :])
    forward_t = match(mm_nt(qb, qa), cots[0:1, :], cots[1:2, :])
    backward_t = match(mm_nt(qa, qb), cots[2:3, :], cots[3:4, :])
    sums_first[...] = mm_tn(forward_t, qb) + mm(backward_t, qb)
    sums_second[...] = mm(forward_t, qa) + mm_tn(backward_t, qa)
    mine = pl.ds(pl.multiple_of(band * 48, 16), 48)
    own_first = sums_first[mine, :]
    own_second = sums_second[mine, :].astype(BF16)
    first[...] = own_first
    joined[0:768, :] = fine_middle[...]
    joined[768:816, :] = own_second[:, 0:128]
    joined[816:864, :] = own_second[:, 128:256]
    hi = own_first.astype(BF16)
    low = (own_first - hi.astype(F32)).astype(BF16)
    f_here = here[band, 0:48, :]
    total = mm_tn(f_here, hi) + mm_tn(f_here, low) + mm_tn(there[band, 0:48, :], own_second)
    packed[:, 0:8, :] = total[:, 0:128].reshape(N_PLANE, 8, 128)
    packed[:, 8:16, :] = total[:, 128:256].reshape(N_PLANE, 8, 128)
    for chunk in range(N_PLANE):
        packed[chunk, 16:20, :] = fine_partial[4 * chunk : 4 * chunk + 4, :]
    send[...] = packed[...][:, 0:20, :].astype(BF16)


def sum_body(parts, out):
    total = parts[0].astype(F32)
    for source in range(1, parts.shape[0]):
        total = total + parts[source].astype(F32)
    rounded = total.astype(BF16)
    for target in range(out.shape[0]):
        out[target] = rounded


def unpack_body(parts, coarse, fine):
    values = parts[...].astype(F32) * (1.0 / N_FRAMES)
    coarse[:, 0:128] = values[:, 0:8, :].reshape(256, 128)
    coarse[:, 128:256] = values[:, 8:16, :].reshape(256, 128)
    for chunk in range(N_PLANE):
        fine[4 * chunk : 4 * chunk + 4, :] = values[chunk, 16:20, :]


def finish_body(first, joined, from_above, from_below, weight, coarse_first, coarse_weight, fine_out, coarse_out):
    total = first[...] + joined[0:768, :].astype(F32)
    w = weight[...]
    top = (total[0:384, :] + from_above[...].astype(F32)).astype(BF16)
    bottom = (total[384:768, :] + from_below[...].astype(F32)).astype(BF16)
    fine_out[0:384, :] = mm_nt(top, w).astype(BF16)
    fine_out[384:768, :] = mm_nt(bottom, w).astype(BF16)
    w = coarse_weight[...]
    left = (coarse_first[:, 0:128] + joined[768:816, :].astype(F32)).astype(BF16)
    right = (coarse_first[:, 128:256] + joined[816:864, :].astype(F32)).astype(BF16)
    coarse_out[...] = (mm_nt(left, w[:, 0:128]) + mm_nt(right, w[:, 128:256])).astype(BF16)


def shifted(value, frames, rows):
    pairs = [
        (f * N_ROWS + r, (f + frames) * N_ROWS + r + rows)
        for f in range(max(0, -frames), min(N_FRAMES, N_FRAMES - frames))
        for r in range(max(0, -rows), min(N_ROWS, N_ROWS - rows))
    ]
    return lax.ppermute(value, ALL, pairs)


def local(coarse_features, fine_features, coarse_weight, fine_weight, grad_refined, grad_back):
    coarse_own = coarse_features.reshape(48, 256)
    fine_own = fine_features.reshape(768, 128)
    refined = grad_refined.reshape(2, 768)
    band = lax.axis_index(ROWS).astype(jnp.int32).reshape(1)
    middle = shifted(fine_own, -1, 0)
    above = shifted(fine_own[384:768], -1, 1)
    below = shifted(fine_own[0:384], -1, -1)
    outgoing = call(
        prepare_body,
        shape(N_ROWS, 64, 256),
        [
            pltpu.VMEM((16, 256), F32),
            pltpu.VMEM((2, 768), F32),
            pltpu.VMEM((2, 48), F32),
            pltpu.SemaphoreType.DMA((N_ROWS + 2,)),
        ],
        n_in=3, flops=10**9, nbytes=10**6, kind=HBM, room=60,
    )(coarse_own, refined, grad_back.reshape(2, 48))
    here = lax.all_to_all(outgoing, ROWS, 0, 0, tiled=True)
    there = shifted(here, -1, 0)
    first, mid_out, up_out, down_out, fine_partial = call(
        fine_body,
        (shape(8, 96, 128, dtype=F32), shape(768, 128), shape(384, 128), shape(384, 128), shape(128, 128, dtype=F32)),
        [
            pltpu.VMEM((8, 96, 128), BF16),
            pltpu.VMEM((16, 128, 128), BF16),
            pltpu.VMEM((16, 128, 128), F32),
            pltpu.VMEM((8, 768), F32),
            pltpu.VMEM((12, 64, 128), F32),
        ],
        n_in=6, flops=20 * 10**9, nbytes=4 * 10**6,
    )(fine_own, middle, above, below, fine_weight, refined)
    back_up = shifted(up_out, 1, -1)
    back_down = shifted(down_out, 1, 1)
    coarse_first, joined, send = call(
        coarse_body,
        (shape(48, 256, dtype=F32), shape(864, 128), shape(N_PLANE, 20, 128)),
        [
            pltpu.VMEM((384, 256), F32),
            pltpu.VMEM((384, 256), F32),
            pltpu.VMEM((N_PLANE, 24, 128), F32),
        ],
        n_smem=1, n_in=5, flops=3 * 10**9, nbytes=2 * 10**6,
    )(band, here, there, coarse_weight, fine_partial, mid_out)
    back_joined = shifted(joined, 1, 0)
    parts = lax.all_to_all(send, PLANE, 0, 0, tiled=True)
    copies = call(sum_body, shape(N_Z, 20, 128), n_in=1, nbytes=10**6)(parts)
    parts = lax.all_to_all(copies, "z", 0, 0, tiled=True)
    parts, back_up, back_joined = lax.optimization_barrier((parts, back_up, back_joined))
    copies = call(sum_body, shape(N_PLANE, 20, 128), n_in=1, nbytes=10**6)(parts)
    parts = lax.all_to_all(copies, PLANE, 0, 0, tiled=True)
    coarse_total, fine_total = call(
        unpack_body, (shape(256, 256, dtype=F32), shape(128, 128, dtype=F32)), n_in=1, nbytes=10**6
    )(parts)
    fine_grad, coarse_grad = call(
        finish_body, (shape(768, 128), shape(48, 256)), n_in=7, flops=10**8, nbytes=10**6
    )(first.reshape(768, 128), back_joined, back_down, back_up, fine_weight, coarse_first, coarse_weight)
    return (
        coarse_grad.reshape(coarse_features.shape),
        fine_grad.reshape(fine_features.shape),
        coarse_total,
        fine_total,
    )


def solution(mesh):
    fine_mesh = Mesh(mesh.devices.reshape(16, 2, 2, 4, 2), ALL)
    in_specs = (
        P(FRAMES, ROWS, None, None),
        P(FRAMES, ROWS, None, None),
        P(),
        P(),
        P(FRAMES, None, ROWS),
        P(FRAMES, None, ROWS),
    )
    out_specs = (P(FRAMES, ROWS, None, None), P(FRAMES, ROWS, None, None), P(), P())
    return jax.shard_map(local, mesh=fine_mesh, in_specs=in_specs, out_specs=out_specs, check_vma=False)
```

```python
import math

import jax
import jax.numpy as jnp
from jax import lax
from jax.experimental import pallas as pl
from jax.experimental.pallas import tpu as pltpu
from jax.sharding import Mesh, PartitionSpec as P

F32 = jnp.float32
BF16 = jnp.bfloat16
FRAMES = ("z", "yh", "core")
ROWS = ("x", "yl")
PLANE = ("yh", "core", "x", "yl")
ALL = FRAMES + ROWS
N_FRAMES, N_ROWS, N_PLANE, N_Z = 64, 8, 32, 16
SOON = 12
VMEM = pl.BlockSpec(memory_space=pltpu.VMEM)
HBM = pl.BlockSpec(memory_space=pltpu.HBM)
SMEM = pl.BlockSpec(memory_space=pltpu.SMEM)


def call(body, outs, scratch=(), n_smem=0, n_in=0, flops=0, nbytes=0, kind=VMEM, room=40):
    return pl.pallas_call(
        body,
        out_shape=outs,
        in_specs=[SMEM] * n_smem + [kind] * n_in,
        out_specs=jax.tree.map(lambda _: VMEM, outs),
        scratch_shapes=list(scratch),
        compiler_params=pltpu.CompilerParams(vmem_limit_bytes=room * 1024 * 1024),
        cost_estimate=pl.CostEstimate(flops=flops, bytes_accessed=nbytes, transcendentals=0),
    )


def shape(*dims, dtype=BF16):
    return jax.ShapeDtypeStruct(dims, dtype)


def mm(a, b):
    return lax.dot_general(a, b, (((1,), (0,)), ((), ())), preferred_element_type=F32)


def mm_nt(a, b):
    return lax.dot_general(a, b, (((1,), (1,)), ((), ())), preferred_element_type=F32)


def mm_tn(a, b):
    return lax.dot_general(a, b, (((0,), (0,)), ((), ())), preferred_element_type=F32)


def split3(value):
    hi = value.astype(BF16)
    rest = value - hi.astype(F32)
    mid = rest.astype(BF16)
    low = (rest - mid.astype(F32)).astype(BF16)
    return hi, mid, low


def iota(dims, axis):
    return lax.broadcasted_iota(jnp.int32, dims, axis)


def prepare_body(coarse_hbm, refined_hbm, back_hbm, out, cots, refined, back, sems):
    copies = [
        pltpu.make_async_copy(refined_hbm, refined, sems.at[N_ROWS]),
        pltpu.make_async_copy(back_hbm, back, sems.at[N_ROWS + 1]),
    ]
    for band in range(N_ROWS):
        copies.append(pltpu.make_async_copy(coarse_hbm, out.at[band, pl.ds(0, 48), :], sems.at[band]))
    for copy in copies:
        copy.start()
    cell = iota((768, 128), 0)
    low = (cell >= 384).astype(jnp.int32)
    cell = cell - 384 * low
    line = (cell >= 96).astype(jnp.int32) + (cell >= 192).astype(jnp.int32) + (cell >= 288).astype(jnp.int32)
    column = lax.shift_right_logical(cell - 96 * line, 2)
    pool = (iota((768, 128), 1) == column + 24 * low).astype(F32).astype(BF16)
    cots[...] = jnp.zeros_like(cots)
    copies[0].wait()
    copies[1].wait()
    hi, mid, rest = split3(refined[...])
    cots[0:2, 0:128] = 4.0 * (mm(hi, pool) + (mm(mid, pool) + mm(rest, pool)))
    cots[2:4, 0:48] = back[...]
    hi, mid, rest = split3(cots[0:4, :])
    cots[0:4, :] = hi.astype(F32)
    cots[4:8, :] = mid.astype(F32)
    cots[8:12, :] = rest.astype(F32)
    packed = cots[...].astype(BF16)
    for band in range(N_ROWS):
        out[band, 48:64, :] = packed
    for copy in copies[2:]:
        copy.wait()


def fine_body(own, middle, above, below, weight, refined, first, mid_out, up_out, down_out, partial,
              queries, keys, key_grad, turned, window):
    scale = 1.0 / math.sqrt(128.0)
    w = weight[...]
    queries[...] = mm(own[...], w).astype(BF16).reshape(8, 96, 128)
    keys[:, 0:16, :] = jnp.zeros((16, 16, 128), BF16)
    keys[:, 112:128, :] = jnp.zeros((16, 16, 128), BF16)
    keys[0:4, 16:112, :] = mm(above[...], w).astype(BF16).reshape(4, 96, 128)
    keys[4:12, 16:112, :] = mm(middle[...], w).astype(BF16).reshape(8, 96, 128)
    keys[12:16, 16:112, :] = mm(below[...], w).astype(BF16).reshape(4, 96, 128)
    key_grad[...] = jnp.zeros_like(key_grad)
    turned[...] = jnp.zeros_like(turned)
    turned[0:2, :] = refined[...]
    upright = jnp.transpose(turned[...], (1, 0))
    lane = iota((1, 128), 1)
    query_x = jnp.bitwise_and(lane, 31).astype(F32)
    query_y = lax.shift_right_logical(lane, 5).astype(F32)
    key_x = iota((64, 128), 0).astype(F32) - 16.0
    near_x = jnp.where(jnp.abs(key_x - query_x) < 4.5, 0.0, -1e30)
    for line in range(12):
        near_y = jnp.where(jnp.abs(line - 4.0 - query_y) < 4.5, 0.0, -1e30)
        window[line] = jnp.minimum(near_x, near_y)
    for part in range(2):
        for column in range(3):
            q = queries[4 * part : 4 * part + 4, 32 * column : 32 * column + 32, :].reshape(128, 128)
            k = keys[4 * part : 4 * part + 12, 32 * column : 32 * column + 64, :].reshape(768, 128)
            pieces = [(4 * part + line) * 96 + 32 * column for line in range(4)]
            cot = jnp.transpose(jnp.concatenate([upright[at : at + 32, :] for at in pieces], axis=0), (1, 0))
            gx, gy = cot[0:1, :], cot[1:2, :]
            s = mm_nt(k, q).reshape(12, 64, 128) * (scale * math.log2(math.e)) + window[...]
            top = jnp.max(jnp.max(s, axis=0), axis=0, keepdims=True)
            e = jnp.exp2(s - top)
            by_x = jnp.sum(e, axis=0)
            inverse = 1.0 / jnp.sum(by_x, axis=0, keepdims=True)
            mean_x = jnp.sum(by_x * key_x, axis=0, keepdims=True) * inverse
            mean_y = jnp.zeros((1, 128), F32)
            for line in range(12):
                mean_y = mean_y + (line - 4.0) * jnp.sum(e[line], axis=0, keepdims=True)
            mean_y = mean_y * inverse
            factor = inverse * scale
            gx, gy = gx * factor, gy * factor
            bend_x = gx * (key_x - mean_x)
            weights = jnp.concatenate(
                [(e[line] * (bend_x + gy * ((line - 4.0) - mean_y))).astype(BF16) for line in range(12)], axis=0
            )
            first[4 * part : 4 * part + 4, 32 * column : 32 * column + 32, :] = mm_tn(weights, k).reshape(4, 32, 128)
            key_grad[4 * part : 4 * part + 12, 32 * column : 32 * column + 64, :] += mm(weights, q).reshape(12, 64, 128)
    up_out[...] = key_grad[0:4, 16:112, :].astype(BF16).reshape(384, 128)
    mid_out[...] = key_grad[4:12, 16:112, :].astype(BF16).reshape(768, 128)
    down_out[...] = key_grad[12:16, 16:112, :].astype(BF16).reshape(384, 128)
    exact = first[...].reshape(768, 128)
    hi = exact.astype(BF16)
    low = (exact - hi.astype(F32)).astype(BF16)
    total = mm_tn(own[...], hi) + mm_tn(own[...], low)
    total = total + mm_tn(middle[...], mid_out[...])
    partial[...] = total + mm_tn(above[...], up_out[...]) + mm_tn(below[...], down_out[...])


def match(scores, cot_x, cot_y):
    s = scores * (math.log2(math.e) / 16.0)
    e = jnp.exp2(s - jnp.max(s, axis=0, keepdims=True)).reshape(16, 24, 384)
    by_x = jnp.sum(e, axis=0)
    inverse = 1.0 / jnp.sum(by_x, axis=0, keepdims=True)
    key_x = iota((24, 384), 0).astype(F32)
    mean_x = jnp.sum(by_x * key_x, axis=0, keepdims=True) * inverse
    mean_y = jnp.zeros((1, 384), F32)
    for line in range(1, 16):
        mean_y = mean_y + float(line) * jnp.sum(e[line], axis=0, keepdims=True)
    mean_y = mean_y * inverse
    factor = inverse * (1.0 / 16.0)
    cot_x, cot_y = cot_x * factor, cot_y * factor
    bend_x = cot_x * (key_x - mean_x)
    lines = [e[line] * (bend_x + cot_y * (float(line) - mean_y)) for line in range(16)]
    return jnp.concatenate(lines, axis=0).astype(BF16)


def coarse_body(position, here, there, weight, fine_partial, fine_middle, first, joined, send,
                sums_first, sums_second, packed):
    band = position[0]
    w = weight[...]
    qa = mm(here[:, 0:48, :].reshape(384, 256), w).astype(BF16)
    qb = mm(there[:, 0:48, :].reshape(384, 256), w).astype(BF16)
    flat = jnp.zeros((16, 384), F32)
    ahead = iota((128, 384), 1) - iota((128, 384), 0)
    for source in range(N_ROWS):
        place = (ahead == 48 * source).astype(F32).astype(BF16)
        flat = flat + mm(here[source, 48:64, 0:128], place)
    cots = flat[0:4, :] + (flat[4:8, :] + flat[8:12, :])
    forward_t = match(mm_nt(qb, qa), cots[0:1, :], cots[1:2, :])
    backward_t = match(mm_nt(qa, qb), cots[2:3, :], cots[3:4, :])
    sums_first[...] = mm_tn(forward_t, qb) + mm(backward_t, qb)
    sums_second[...] = mm(forward_t, qa) + mm_tn(backward_t, qa)
    mine = pl.ds(pl.multiple_of(band * 48, 16), 48)
    own_first = sums_first[mine, :]
    own_second = sums_second[mine, :].astype(BF16)
    first[...] = own_first
    joined[0:768, :] = fine_middle[...]
    joined[768:816, :] = own_second[:, 0:128]
    joined[816:864, :] = own_second[:, 128:256]
    hi = own_first.astype(BF16)
    low = (own_first - hi.astype(F32)).astype(BF16)
    f_here = here[band, 0:48, :]
    total = mm_tn(f_here, hi) + mm_tn(f_here, low) + mm_tn(there[band, 0:48, :], own_second)
    packed[:, 0:8, :] = total[:, 0:128].reshape(N_PLANE, 8, 128)
    packed[:, 8:16, :] = total[:, 128:256].reshape(N_PLANE, 8, 128)
    for chunk in range(N_PLANE):
        packed[chunk, 16:20, :] = fine_partial[4 * chunk : 4 * chunk + 4, :]
    send[...] = packed[...][:, 0:20, :].astype(BF16)


def sum_body(parts, out):
    total = parts[0].astype(F32)
    for source in range(1, parts.shape[0]):
        total = total + parts[source].astype(F32)
    rounded = total.astype(BF16)
    for target in range(out.shape[0]):
        out[target] = rounded


def unpack_body(parts, coarse, fine):
    values = parts[...].astype(F32) * (1.0 / N_FRAMES)
    coarse[:, 0:128] = values[:, 0:8, :].reshape(256, 128)
    coarse[:, 128:256] = values[:, 8:16, :].reshape(256, 128)
    for chunk in range(N_PLANE):
        fine[4 * chunk : 4 * chunk + 4, :] = values[chunk, 16:20, :]


def finish_body(first, joined, above_soon, above_late, below_soon, below_late, weight, coarse_first, coarse_weight, fine_out, coarse_out):
    total = first[...] + joined[0:768, :].astype(F32)
    w = weight[...]
    top = (total[0:384, :] + (above_soon[...].astype(F32) + above_late[...].astype(F32))).astype(BF16)
    bottom = (total[384:768, :] + (below_soon[...].astype(F32) + below_late[...].astype(F32))).astype(BF16)
    fine_out[0:384, :] = mm_nt(top, w).astype(BF16)
    fine_out[384:768, :] = mm_nt(bottom, w).astype(BF16)
    w = coarse_weight[...]
    left = (coarse_first[:, 0:128] + joined[768:816, :].astype(F32)).astype(BF16)
    right = (coarse_first[:, 128:256] + joined[816:864, :].astype(F32)).astype(BF16)
    coarse_out[...] = (mm_nt(left, w[:, 0:128]) + mm_nt(right, w[:, 128:256])).astype(BF16)


def shifted(value, frames, rows, sources=(0, N_FRAMES)):
    pairs = [
        (f * N_ROWS + r, (f + frames) * N_ROWS + r + rows)
        for f in range(max(sources[0], -frames), min(sources[1], N_FRAMES - frames))
        for r in range(max(0, -rows), min(N_ROWS, N_ROWS - rows))
    ]
    return lax.ppermute(value, ALL, pairs)


def local(coarse_features, fine_features, coarse_weight, fine_weight, grad_refined, grad_back):
    coarse_own = coarse_features.reshape(48, 256)
    fine_own = fine_features.reshape(768, 128)
    refined = grad_refined.reshape(2, 768)
    band = lax.axis_index(ROWS).astype(jnp.int32).reshape(1)
    middle = shifted(fine_own, -1, 0)
    above = shifted(fine_own[384:768], -1, 1)
    below = shifted(fine_own[0:384], -1, -1)
    outgoing = call(
        prepare_body,
        shape(N_ROWS, 64, 256),
        [
            pltpu.VMEM((16, 256), F32),
            pltpu.VMEM((2, 768), F32),
            pltpu.VMEM((2, 48), F32),
            pltpu.SemaphoreType.DMA((N_ROWS + 2,)),
        ],
        n_in=3, flops=10**9, nbytes=10**6, kind=HBM, room=60,
    )(coarse_own, refined, grad_back.reshape(2, 48))
    here = lax.all_to_all(outgoing, ROWS, 0, 0, tiled=True)
    there = shifted(here, -1, 0)
    first, mid_out, up_out, down_out, fine_partial = call(
        fine_body,
        (shape(8, 96, 128, dtype=F32), shape(768, 128), shape(384, 128), shape(384, 128), shape(128, 128, dtype=F32)),
        [
            pltpu.VMEM((8, 96, 128), BF16),
            pltpu.VMEM((16, 128, 128), BF16),
            pltpu.VMEM((16, 128, 128), F32),
            pltpu.VMEM((8, 768), F32),
            pltpu.VMEM((12, 64, 128), F32),
        ],
        n_in=6, flops=20 * 10**9, nbytes=4 * 10**6,
    )(fine_own, middle, above, below, fine_weight, refined)
    back_up_soon, back_up = (shifted(up_out, 1, -1, part) for part in ((0, SOON), (SOON, N_FRAMES)))
    back_down_soon, back_down = (shifted(down_out, 1, 1, part) for part in ((0, SOON), (SOON, N_FRAMES)))
    coarse_first, joined, send = call(
        coarse_body,
        (shape(48, 256, dtype=F32), shape(864, 128), shape(N_PLANE, 20, 128)),
        [
            pltpu.VMEM((384, 256), F32),
            pltpu.VMEM((384, 256), F32),
            pltpu.VMEM((N_PLANE, 24, 128), F32),
        ],
        n_smem=1, n_in=5, flops=3 * 10**9, nbytes=2 * 10**6,
    )(band, here, there, coarse_weight, fine_partial, mid_out)
    back_joined = shifted(joined, 1, 0)
    parts = lax.all_to_all(send, PLANE, 0, 0, tiled=True)
    parts, back_up_soon, back_down_soon = lax.optimization_barrier((parts, back_up_soon, back_down_soon))
    copies = call(sum_body, shape(N_Z, 20, 128), n_in=1, nbytes=10**6)(parts)
    parts = lax.all_to_all(copies, "z", 0, 0, axis_index_groups=[[(9 + i) % N_Z for i in range(N_Z)]], tiled=True)
    copies = call(sum_body, shape(N_PLANE, 20, 128), n_in=1, nbytes=10**6)(parts)
    parts = lax.all_to_all(copies, PLANE, 0, 0, tiled=True)
    coarse_total, fine_total = call(
        unpack_body, (shape(256, 256, dtype=F32), shape(128, 128, dtype=F32)), n_in=1, nbytes=10**6
    )(parts)
    fine_grad, coarse_grad = call(
        finish_body, (shape(768, 128), shape(48, 256)), n_in=9, flops=20 * 10**9, nbytes=10**6
    )(first.reshape(768, 128), back_joined, back_down_soon, back_down, back_up_soon, back_up, fine_weight, coarse_first, coarse_weight)
    return (
        coarse_grad.reshape(coarse_features.shape),
        fine_grad.reshape(fine_features.shape),
        coarse_total,
        fine_total,
    )


def solution(mesh):
    fine_mesh = Mesh(mesh.devices.reshape(16, 2, 2, 4, 2), ALL)
    in_specs = (
        P(FRAMES, ROWS, None, None),
        P(FRAMES, ROWS, None, None),
        P(),
        P(),
        P(FRAMES, None, ROWS),
        P(FRAMES, None, ROWS),
    )
    out_specs = (P(FRAMES, ROWS, None, None), P(FRAMES, ROWS, None, None), P(), P())
    return jax.shard_map(local, mesh=fine_mesh, in_specs=in_specs, out_specs=out_specs, check_vma=False)
```

```python
import math

import jax
import jax.numpy as jnp
from jax import lax
from jax.experimental import pallas as pl
from jax.experimental.pallas import tpu as pltpu
from jax.sharding import Mesh, PartitionSpec as P

F32 = jnp.float32
BF16 = jnp.bfloat16
FRAMES = ("z", "yh", "core")
ROWS = ("x", "yl")
PLANE = ("yh", "core", "x", "yl")
ALL = FRAMES + ROWS
N_FRAMES, N_ROWS, N_PLANE, N_Z = 64, 8, 32, 16
VMEM = pl.BlockSpec(memory_space=pltpu.VMEM)
HBM = pl.BlockSpec(memory_space=pltpu.HBM)


def call(body, outs, scratch=(), n_in=0, flops=0, nbytes=0, kind=VMEM, room=40):
    return pl.pallas_call(
        body,
        out_shape=outs,
        in_specs=[kind] * n_in,
        out_specs=jax.tree.map(lambda _: VMEM, outs),
        scratch_shapes=list(scratch),
        compiler_params=pltpu.CompilerParams(vmem_limit_bytes=room * 1024 * 1024),
        cost_estimate=pl.CostEstimate(flops=flops, bytes_accessed=nbytes, transcendentals=0),
    )


def shape(*dims, dtype=BF16):
    return jax.ShapeDtypeStruct(dims, dtype)


def mm(a, b):
    return lax.dot_general(a, b, (((1,), (0,)), ((), ())), preferred_element_type=F32)


def mm_nt(a, b):
    return lax.dot_general(a, b, (((1,), (1,)), ((), ())), preferred_element_type=F32)


def mm_tn(a, b):
    return lax.dot_general(a, b, (((0,), (0,)), ((), ())), preferred_element_type=F32)


def split3(value):
    hi = value.astype(BF16)
    rest = value - hi.astype(F32)
    mid = rest.astype(BF16)
    low = (rest - mid.astype(F32)).astype(BF16)
    return hi, mid, low


def iota(dims, axis):
    return lax.broadcasted_iota(jnp.int32, dims, axis)


def key_frame_present():
    frame = (lax.axis_index("z") * 2 + lax.axis_index("yh")) * 2 + lax.axis_index("core")
    return jnp.minimum(frame, 1).astype(F32)


def prepare_body(coarse_hbm, fine_hbm, refined_hbm, back_hbm, out, taken, cots, refined, back, sems):
    copies = [
        pltpu.make_async_copy(refined_hbm, refined, sems.at[N_ROWS]),
        pltpu.make_async_copy(back_hbm, back, sems.at[N_ROWS + 1]),
        pltpu.make_async_copy(fine_hbm, taken.at[pl.ds(0, 768), :], sems.at[N_ROWS + 2]),
    ]
    for band in range(N_ROWS):
        copies.append(pltpu.make_async_copy(coarse_hbm, out.at[band, pl.ds(0, 48), :], sems.at[band]))
    for copy in copies:
        copy.start()
    cell = iota((768, 128), 0)
    low = (cell >= 384).astype(jnp.int32)
    cell = cell - 384 * low
    line = (cell >= 96).astype(jnp.int32) + (cell >= 192).astype(jnp.int32) + (cell >= 288).astype(jnp.int32)
    column = lax.shift_right_logical(cell - 96 * line, 2)
    pool = (iota((768, 128), 1) == column + 24 * low).astype(F32).astype(BF16)
    cots[...] = jnp.zeros_like(cots)
    copies[0].wait()
    copies[1].wait()
    terms = split3(refined[...])
    for term in range(3):
        wide = terms[term].astype(F32)
        for k in range(6):
            at = 16 + 16 * term + 2 * k
            cots[at : at + 2, 0:128] = wide[:, 128 * k : 128 * k + 128]
    cots[0:2, 0:128] = 4.0 * (mm(terms[0], pool) + (mm(terms[1], pool) + mm(terms[2], pool)))
    cots[2:4, 0:48] = back[...]
    hi, mid, rest = split3(cots[0:4, :])
    cots[0:4, :] = hi.astype(F32)
    cots[4:8, :] = mid.astype(F32)
    cots[8:12, :] = rest.astype(F32)
    packed = cots[0:16, :].astype(BF16)
    taken[768:816, :] = cots[16:64, 0:128].astype(BF16)
    for band in range(N_ROWS):
        out[band, 48:64, :] = packed
    for copy in copies[2:]:
        copy.wait()


def fine_body(taken, own, above, below, weight, first_out, mid_out, up_out, down_out, partial,
              first, queries, keys, key_grad, turned, window):
    scale = 1.0 / math.sqrt(128.0)
    w = weight[...]
    present = key_frame_present()
    queries[...] = mm(taken[0:768, :], w).astype(BF16).reshape(8, 96, 128)
    keys[:, 0:16, :] = jnp.zeros((16, 16, 128), BF16)
    keys[:, 112:128, :] = jnp.zeros((16, 16, 128), BF16)
    keys[0:4, 16:112, :] = (mm(above[...], w) * present).astype(BF16).reshape(4, 96, 128)
    keys[4:12, 16:112, :] = (mm(own[...], w) * present).astype(BF16).reshape(8, 96, 128)
    keys[12:16, 16:112, :] = (mm(below[...], w) * present).astype(BF16).reshape(4, 96, 128)
    key_grad[...] = jnp.zeros_like(key_grad)
    turned[...] = jnp.zeros_like(turned)
    terms = taken[768:816, :].astype(F32)
    refined = terms[0:16, :] + (terms[16:32, :] + terms[32:48, :])
    for k in range(6):
        turned[0:2, 128 * k : 128 * k + 128] = refined[2 * k : 2 * k + 2, :]
    upright = jnp.transpose(turned[...], (1, 0))
    lane = iota((1, 128), 1)
    query_x = jnp.bitwise_and(lane, 31).astype(F32)
    query_y = lax.shift_right_logical(lane, 5).astype(F32)
    key_x = iota((64, 128), 0).astype(F32) - 16.0
    near_x = jnp.where(jnp.abs(key_x - query_x) < 4.5, 0.0, -1e30)
    for line in range(12):
        near_y = jnp.where(jnp.abs(line - 4.0 - query_y) < 4.5, 0.0, -1e30)
        window[line] = jnp.minimum(near_x, near_y)
    for part in range(2):
        for column in range(3):
            q = queries[4 * part : 4 * part + 4, 32 * column : 32 * column + 32, :].reshape(128, 128)
            k = keys[4 * part : 4 * part + 12, 32 * column : 32 * column + 64, :].reshape(768, 128)
            pieces = [(4 * part + line) * 96 + 32 * column for line in range(4)]
            cot = jnp.transpose(jnp.concatenate([upright[at : at + 32, :] for at in pieces], axis=0), (1, 0))
            gx, gy = cot[0:1, :], cot[1:2, :]
            s = mm_nt(k, q).reshape(12, 64, 128) * (scale * math.log2(math.e)) + window[...]
            top = jnp.max(jnp.max(s, axis=0), axis=0, keepdims=True)
            e = jnp.exp2(s - top)
            by_x = jnp.sum(e, axis=0)
            inverse = 1.0 / jnp.sum(by_x, axis=0, keepdims=True)
            mean_x = jnp.sum(by_x * key_x, axis=0, keepdims=True) * inverse
            mean_y = jnp.zeros((1, 128), F32)
            for line in range(12):
                mean_y = mean_y + (line - 4.0) * jnp.sum(e[line], axis=0, keepdims=True)
            mean_y = mean_y * inverse
            factor = inverse * scale
            gx, gy = gx * factor, gy * factor
            bend_x = gx * (key_x - mean_x)
            weights = jnp.concatenate(
                [(e[line] * (bend_x + gy * ((line - 4.0) - mean_y))).astype(BF16) for line in range(12)], axis=0
            )
            first[4 * part : 4 * part + 4, 32 * column : 32 * column + 32, :] = mm_tn(weights, k).reshape(4, 32, 128)
            key_grad[4 * part : 4 * part + 12, 32 * column : 32 * column + 64, :] += mm(weights, q).reshape(12, 64, 128)
    up_out[...] = (key_grad[0:4, 16:112, :] * present).astype(BF16).reshape(384, 128)
    mid_out[...] = (key_grad[4:12, 16:112, :] * present).astype(BF16).reshape(768, 128)
    down_out[...] = (key_grad[12:16, 16:112, :] * present).astype(BF16).reshape(384, 128)
    exact = first[...].reshape(768, 128)
    hi = exact.astype(BF16)
    low = (exact - hi.astype(F32)).astype(BF16)
    first_out[...] = exact
    total = mm_tn(taken[0:768, :], hi) + mm_tn(taken[0:768, :], low)
    total = total + mm_tn(own[...], mid_out[...])
    partial[...] = total + mm_tn(above[...], up_out[...]) + mm_tn(below[...], down_out[...])


def match(scores, cot_x, cot_y):
    s = scores * (math.log2(math.e) / 16.0)
    e = jnp.exp2(s - jnp.max(s, axis=0, keepdims=True)).reshape(16, 24, 384)
    by_x = jnp.sum(e, axis=0)
    inverse = 1.0 / jnp.sum(by_x, axis=0, keepdims=True)
    key_x = iota((24, 384), 0).astype(F32)
    mean_x = jnp.sum(by_x * key_x, axis=0, keepdims=True) * inverse
    mean_y = jnp.zeros((1, 384), F32)
    for line in range(1, 16):
        mean_y = mean_y + float(line) * jnp.sum(e[line], axis=0, keepdims=True)
    mean_y = mean_y * inverse
    factor = inverse * (1.0 / 16.0)
    cot_x, cot_y = cot_x * factor, cot_y * factor
    bend_x = cot_x * (key_x - mean_x)
    lines = [e[line] * (bend_x + cot_y * (float(line) - mean_y)) for line in range(16)]
    return jnp.concatenate(lines, axis=0).astype(BF16)


def coarse_body(before, own, weight, fine_partial, fine_first, second, joined, send,
                sums_first, sums_second, packed):
    band, present = lax.axis_index("x") * 2 + lax.axis_index("yl"), key_frame_present()
    w = weight[...]
    qa = mm(before[:, 0:48, :].reshape(384, 256), w).astype(BF16)
    qb = (mm(own[:, 0:48, :].reshape(384, 256), w) * present).astype(BF16)
    flat = jnp.zeros((16, 384), F32)
    ahead = iota((128, 384), 1) - iota((128, 384), 0)
    for source in range(N_ROWS):
        place = (ahead == 48 * source).astype(F32).astype(BF16)
        flat = flat + mm(before[source, 48:64, 0:128], place)
    cots = flat[0:4, :] + (flat[4:8, :] + flat[8:12, :])
    forward_t = match(mm_nt(qb, qa), cots[0:1, :], cots[1:2, :])
    backward_t = match(mm_nt(qa, qb), cots[2:3, :], cots[3:4, :])
    sums_first[...] = mm_tn(forward_t, qb) + mm(backward_t, qb)
    sums_second[...] = mm(forward_t, qa) + mm_tn(backward_t, qa)
    mine = pl.ds(pl.multiple_of(band * 48, 16), 48)
    own_first = sums_first[mine, :]
    own_second = (sums_second[mine, :] * present).astype(BF16)
    second[...] = own_second
    hi = own_first.astype(BF16)
    low = (own_first - hi.astype(F32)).astype(BF16)
    joined[0:768, :] = fine_first[...]
    joined[768:816, :] = own_first[:, 0:128]
    joined[816:864, :] = own_first[:, 128:256]
    f_before = before[band, 0:48, :]
    total = mm_tn(f_before, hi) + mm_tn(f_before, low) + mm_tn(own[band, 0:48, :], own_second)
    packed[:, 0:8, :] = total[:, 0:128].reshape(N_PLANE, 8, 128)
    packed[:, 8:16, :] = total[:, 128:256].reshape(N_PLANE, 8, 128)
    for chunk in range(N_PLANE):
        packed[chunk, 16:20, :] = fine_partial[4 * chunk : 4 * chunk + 4, :]
    send[...] = packed[...][:, 0:20, :].astype(BF16)


def sum_body(parts, out):
    total = parts[0].astype(F32)
    for source in range(1, parts.shape[0]):
        total = total + parts[source].astype(F32)
    rounded = total.astype(BF16)
    for target in range(out.shape[0]):
        out[target] = rounded


def unpack_body(parts, coarse, fine):
    values = parts[...].astype(F32) * (1.0 / N_FRAMES)
    coarse[:, 0:128] = values[:, 0:8, :].reshape(256, 128)
    coarse[:, 128:256] = values[:, 8:16, :].reshape(256, 128)
    for chunk in range(N_PLANE):
        fine[4 * chunk : 4 * chunk + 4, :] = values[chunk, 16:20, :]


def finish_body(returned, middle, from_above, from_below, weight, coarse_second, coarse_weight, fine_out, coarse_out):
    w = weight[...]
    total = returned[0:768, :] + middle[...].astype(F32)
    top = (total[0:384, :] + from_above[...].astype(F32)).astype(BF16)
    bottom = (total[384:768, :] + from_below[...].astype(F32)).astype(BF16)
    fine_out[0:384, :] = mm_nt(top, w).astype(BF16)
    fine_out[384:768, :] = mm_nt(bottom, w).astype(BF16)
    w = coarse_weight[...]
    second = coarse_second[...].astype(F32)
    left = (returned[768:816, :] + second[:, 0:128]).astype(BF16)
    right = (returned[816:864, :] + second[:, 128:256]).astype(BF16)
    coarse_out[...] = (mm_nt(left, w[:, 0:128]) + mm_nt(right, w[:, 128:256])).astype(BF16)


def shifted(value, frames, rows):
    pairs = [
        (f * N_ROWS + r, (f + frames) % N_FRAMES * N_ROWS + r + rows)
        for f in range(N_FRAMES)
        for r in range(max(0, -rows), min(N_ROWS, N_ROWS - rows))
    ]
    return lax.ppermute(value, ALL, pairs)


def local(coarse_features, fine_features, coarse_weight, fine_weight, grad_refined, grad_back):
    coarse_own = coarse_features.reshape(48, 256)
    fine_own = fine_features.reshape(768, 128)
    above = shifted(fine_own[384:768], 0, 1)
    below = shifted(fine_own[0:384], 0, -1)
    outgoing, taken = call(
        prepare_body,
        (shape(N_ROWS, 64, 256), shape(816, 128)),
        [
            pltpu.VMEM((64, 256), F32),
            pltpu.VMEM((2, 768), F32),
            pltpu.VMEM((2, 48), F32),
            pltpu.SemaphoreType.DMA((N_ROWS + 3,)),
        ],
        n_in=4, flops=10**9, nbytes=10**6, kind=HBM, room=60,
    )(coarse_own, fine_own, grad_refined.reshape(2, 768), grad_back.reshape(2, 48))
    taken = shifted(taken, 1, 0)
    own = lax.all_to_all(outgoing, ROWS, 0, 0, tiled=True)
    before = shifted(own, 1, 0)
    fine_first, middle, up_out, down_out, fine_partial = call(
        fine_body,
        (shape(768, 128, dtype=F32), shape(768, 128), shape(384, 128), shape(384, 128), shape(128, 128, dtype=F32)),
        [
            pltpu.VMEM((8, 96, 128), F32),
            pltpu.VMEM((8, 96, 128), BF16),
            pltpu.VMEM((16, 128, 128), BF16),
            pltpu.VMEM((16, 128, 128), F32),
            pltpu.VMEM((8, 768), F32),
            pltpu.VMEM((12, 64, 128), F32),
        ],
        n_in=5, flops=20 * 10**9, nbytes=4 * 10**6,
    )(taken, fine_own, above, below, fine_weight)
    back_up = shifted(up_out, 0, -1)
    back_down = shifted(down_out, 0, 1)
    coarse_second, joined, send = call(
        coarse_body,
        (shape(48, 256), shape(864, 128, dtype=F32), shape(N_PLANE, 20, 128)),
        [
            pltpu.VMEM((384, 256), F32),
            pltpu.VMEM((384, 256), F32),
            pltpu.VMEM((N_PLANE, 24, 128), F32),
        ],
        n_in=5, flops=3 * 10**9, nbytes=2 * 10**6,
    )(before, own, coarse_weight, fine_partial, fine_first)
    returned = shifted(joined, -1, 0)
    parts = lax.all_to_all(send, PLANE, 0, 0, tiled=True)
    copies = call(sum_body, shape(N_Z, 20, 128), n_in=1, nbytes=10**6)(parts)
    parts = lax.all_to_all(copies, "z", 0, 0, axis_index_groups=[[(9 + i) % N_Z for i in range(N_Z)]], tiled=True)
    copies = call(sum_body, shape(N_PLANE, 20, 128), n_in=1, nbytes=10**6)(parts)
    parts = lax.all_to_all(copies, PLANE, 0, 0, tiled=True)
    coarse_total, fine_total = call(
        unpack_body, (shape(256, 256, dtype=F32), shape(128, 128, dtype=F32)), n_in=1, nbytes=10**6
    )(parts)
    fine_grad, coarse_grad = call(
        finish_body, (shape(768, 128), shape(48, 256)), n_in=7, flops=20 * 10**9, nbytes=10**6
    )(returned, middle, back_down, back_up, fine_weight, coarse_second, coarse_weight)
    return (
        coarse_grad.reshape(coarse_features.shape),
        fine_grad.reshape(fine_features.shape),
        coarse_total,
        fine_total,
    )


def solution(mesh):
    fine_mesh = Mesh(mesh.devices.reshape(16, 2, 2, 4, 2), ALL)
    in_specs = (
        P(FRAMES, ROWS, None, None),
        P(FRAMES, ROWS, None, None),
        P(),
        P(),
        P(FRAMES, None, ROWS),
        P(FRAMES, None, ROWS),
    )
    out_specs = (P(FRAMES, ROWS, None, None), P(FRAMES, ROWS, None, None), P(), P())
    return jax.shard_map(local, mesh=fine_mesh, in_specs=in_specs, out_specs=out_specs, check_vma=False)
```

```python
import math

import jax
import jax.numpy as jnp
from jax import lax
from jax.experimental import pallas as pl
from jax.experimental.pallas import tpu as pltpu
from jax.sharding import Mesh, PartitionSpec as P

F32 = jnp.float32
BF16 = jnp.bfloat16
FRAMES = ("z", "yh", "core")
ROWS = ("x", "yl")
PLANE = ("yh", "core", "x", "yl")
ALL = FRAMES + ROWS
N_FRAMES, N_ROWS, N_PLANE, N_Z = 64, 8, 32, 16
VMEM = pl.BlockSpec(memory_space=pltpu.VMEM)
HBM = pl.BlockSpec(memory_space=pltpu.HBM)


def call(body, outs, scratch=(), n_in=0, flops=0, nbytes=0, kind=VMEM, room=40):
    return pl.pallas_call(
        body,
        out_shape=outs,
        in_specs=[kind] * n_in,
        out_specs=jax.tree.map(lambda _: VMEM, outs),
        scratch_shapes=list(scratch),
        compiler_params=pltpu.CompilerParams(vmem_limit_bytes=room * 1024 * 1024),
        cost_estimate=pl.CostEstimate(flops=flops, bytes_accessed=nbytes, transcendentals=0),
    )


def shape(*dims, dtype=BF16):
    return jax.ShapeDtypeStruct(dims, dtype)


def mm(a, b):
    return lax.dot_general(a, b, (((1,), (0,)), ((), ())), preferred_element_type=F32)


def mm_nt(a, b):
    return lax.dot_general(a, b, (((1,), (1,)), ((), ())), preferred_element_type=F32)


def mm_tn(a, b):
    return lax.dot_general(a, b, (((0,), (0,)), ((), ())), preferred_element_type=F32)


def split3(value):
    hi = value.astype(BF16)
    rest = value - hi.astype(F32)
    mid = rest.astype(BF16)
    low = (rest - mid.astype(F32)).astype(BF16)
    return hi, mid, low


def iota(dims, axis):
    return lax.broadcasted_iota(jnp.int32, dims, axis)


def key_frame_present():
    frame = (lax.axis_index("z") * 2 + lax.axis_index("yh")) * 2 + lax.axis_index("core")
    return jnp.minimum(frame, 1).astype(F32)


def prepare_body(coarse_hbm, fine_hbm, refined_hbm, back_hbm, taken, cots, coarse, refined, back, sems):
    copies = [
        pltpu.make_async_copy(refined_hbm, refined, sems.at[0]),
        pltpu.make_async_copy(back_hbm, back, sems.at[1]),
        pltpu.make_async_copy(coarse_hbm, coarse, sems.at[2]),
        pltpu.make_async_copy(fine_hbm, taken.at[pl.ds(0, 768), :], sems.at[3]),
    ]
    for copy in copies:
        copy.start()
    cell = iota((768, 128), 0)
    low = (cell >= 384).astype(jnp.int32)
    cell = cell - 384 * low
    line = (cell >= 96).astype(jnp.int32) + (cell >= 192).astype(jnp.int32) + (cell >= 288).astype(jnp.int32)
    column = lax.shift_right_logical(cell - 96 * line, 2)
    pool = (iota((768, 128), 1) == column + 24 * low).astype(F32).astype(BF16)
    cots[...] = jnp.zeros_like(cots)
    copies[0].wait()
    copies[1].wait()
    terms = split3(refined[...])
    for term in range(3):
        wide = terms[term].astype(F32)
        for k in range(6):
            at = 16 * term + 2 * k
            cots[at : at + 2, :] = wide[:, 128 * k : 128 * k + 128]
    cots[48:50, :] = 4.0 * (mm(terms[0], pool) + (mm(terms[1], pool) + mm(terms[2], pool)))
    cots[50:52, 0:48] = back[...]
    hi, mid, rest = split3(cots[48:52, :])
    cots[48:52, :] = hi.astype(F32)
    cots[52:56, :] = mid.astype(F32)
    cots[56:60, :] = rest.astype(F32)
    taken[864:928, :] = cots[...].astype(BF16)
    copies[2].wait()
    taken[768:816, :] = coarse[:, 0:128]
    taken[816:864, :] = coarse[:, 128:256]
    copies[3].wait()


def pack_body(coarse, taken, out):
    before = jnp.concatenate([taken[768:816, :], taken[816:864, :]], axis=1)
    cots = jnp.concatenate([taken[912:928, :], jnp.zeros((16, 128), BF16)], axis=1)
    for band in range(N_ROWS):
        out[band, 0:48, :] = coarse[...]
        out[band, 48:96, :] = before
        out[band, 96:112, :] = cots


def fine_body(taken, own, above, below, weight, first_out, mid_out, up_out, down_out, partial,
              first, queries, keys, key_grad, turned, window):
    scale = 1.0 / math.sqrt(128.0)
    w = weight[...]
    present = key_frame_present()
    queries[...] = mm(taken[0:768, :], w).astype(BF16).reshape(8, 96, 128)
    keys[:, 0:16, :] = jnp.zeros((16, 16, 128), BF16)
    keys[:, 112:128, :] = jnp.zeros((16, 16, 128), BF16)
    keys[0:4, 16:112, :] = (mm(above[...], w) * present).astype(BF16).reshape(4, 96, 128)
    keys[4:12, 16:112, :] = (mm(own[...], w) * present).astype(BF16).reshape(8, 96, 128)
    keys[12:16, 16:112, :] = (mm(below[...], w) * present).astype(BF16).reshape(4, 96, 128)
    key_grad[...] = jnp.zeros_like(key_grad)
    turned[...] = jnp.zeros_like(turned)
    terms = taken[864:912, :].astype(F32)
    refined = terms[0:16, :] + (terms[16:32, :] + terms[32:48, :])
    for k in range(6):
        turned[0:2, 128 * k : 128 * k + 128] = refined[2 * k : 2 * k + 2, :]
    upright = jnp.transpose(turned[...], (1, 0))
    lane = iota((1, 128), 1)
    query_x = jnp.bitwise_and(lane, 31).astype(F32)
    query_y = lax.shift_right_logical(lane, 5).astype(F32)
    key_x = iota((64, 128), 0).astype(F32) - 16.0
    near_x = jnp.where(jnp.abs(key_x - query_x) < 4.5, 0.0, -1e30)
    for line in range(12):
        near_y = jnp.where(jnp.abs(line - 4.0 - query_y) < 4.5, 0.0, -1e30)
        window[line] = jnp.minimum(near_x, near_y)
    for part in range(2):
        for column in range(3):
            q = queries[4 * part : 4 * part + 4, 32 * column : 32 * column + 32, :].reshape(128, 128)
            k = keys[4 * part : 4 * part + 12, 32 * column : 32 * column + 64, :].reshape(768, 128)
            pieces = [(4 * part + line) * 96 + 32 * column for line in range(4)]
            cot = jnp.transpose(jnp.concatenate([upright[at : at + 32, :] for at in pieces], axis=0), (1, 0))
            gx, gy = cot[0:1, :], cot[1:2, :]
            s = mm_nt(k, q).reshape(12, 64, 128) * (scale * math.log2(math.e)) + window[...]
            top = jnp.max(jnp.max(s, axis=0), axis=0, keepdims=True)
            e = jnp.exp2(s - top)
            by_x = jnp.sum(e, axis=0)
            inverse = 1.0 / jnp.sum(by_x, axis=0, keepdims=True)
            mean_x = jnp.sum(by_x * key_x, axis=0, keepdims=True) * inverse
            mean_y = jnp.zeros((1, 128), F32)
            for line in range(12):
                mean_y = mean_y + (line - 4.0) * jnp.sum(e[line], axis=0, keepdims=True)
            mean_y = mean_y * inverse
            factor = inverse * scale
            gx, gy = gx * factor, gy * factor
            bend_x = gx * (key_x - mean_x)
            weights = jnp.concatenate(
                [(e[line] * (bend_x + gy * ((line - 4.0) - mean_y))).astype(BF16) for line in range(12)], axis=0
            )
            first[4 * part : 4 * part + 4, 32 * column : 32 * column + 32, :] = mm_tn(weights, k).reshape(4, 32, 128)
            key_grad[4 * part : 4 * part + 12, 32 * column : 32 * column + 64, :] += mm(weights, q).reshape(12, 64, 128)
    up_out[...] = (key_grad[0:4, 16:112, :] * present).astype(BF16).reshape(384, 128)
    mid_out[...] = (key_grad[4:12, 16:112, :] * present).astype(BF16).reshape(768, 128)
    down_out[...] = (key_grad[12:16, 16:112, :] * present).astype(BF16).reshape(384, 128)
    exact = first[...].reshape(768, 128)
    hi = exact.astype(BF16)
    low = (exact - hi.astype(F32)).astype(BF16)
    first_out[...] = exact
    total = mm_tn(taken[0:768, :], hi) + mm_tn(taken[0:768, :], low)
    total = total + mm_tn(own[...], mid_out[...])
    partial[...] = total + mm_tn(above[...], up_out[...]) + mm_tn(below[...], down_out[...])


def match(scores, cot_x, cot_y):
    s = scores * (math.log2(math.e) / 16.0)
    e = jnp.exp2(s - jnp.max(s, axis=0, keepdims=True)).reshape(16, 24, 384)
    by_x = jnp.sum(e, axis=0)
    inverse = 1.0 / jnp.sum(by_x, axis=0, keepdims=True)
    key_x = iota((24, 384), 0).astype(F32)
    mean_x = jnp.sum(by_x * key_x, axis=0, keepdims=True) * inverse
    mean_y = jnp.zeros((1, 384), F32)
    for line in range(1, 16):
        mean_y = mean_y + float(line) * jnp.sum(e[line], axis=0, keepdims=True)
    mean_y = mean_y * inverse
    factor = inverse * (1.0 / 16.0)
    cot_x, cot_y = cot_x * factor, cot_y * factor
    bend_x = cot_x * (key_x - mean_x)
    lines = [e[line] * (bend_x + cot_y * (float(line) - mean_y)) for line in range(16)]
    return jnp.concatenate(lines, axis=0).astype(BF16)


def coarse_body(bands, weight, fine_partial, fine_first, second, joined, send,
                sums_first, sums_second, packed):
    band, present = lax.axis_index("x") * 2 + lax.axis_index("yl"), key_frame_present()
    w = weight[...]
    qa = mm(bands[:, 48:96, :].reshape(384, 256), w).astype(BF16)
    qb = (mm(bands[:, 0:48, :].reshape(384, 256), w) * present).astype(BF16)
    flat = jnp.zeros((16, 384), F32)
    ahead = iota((128, 384), 1) - iota((128, 384), 0)
    for source in range(N_ROWS):
        place = (ahead == 48 * source).astype(F32).astype(BF16)
        flat = flat + mm(bands[source, 96:112, 0:128], place)
    cots = flat[0:4, :] + (flat[4:8, :] + flat[8:12, :])
    forward_t = match(mm_nt(qb, qa), cots[0:1, :], cots[1:2, :])
    backward_t = match(mm_nt(qa, qb), cots[2:3, :], cots[3:4, :])
    sums_first[...] = mm_tn(forward_t, qb) + mm(backward_t, qb)
    sums_second[...] = mm(forward_t, qa) + mm_tn(backward_t, qa)
    mine = pl.ds(pl.multiple_of(band * 48, 16), 48)
    own_first = sums_first[mine, :]
    own_second = (sums_second[mine, :] * present).astype(BF16)
    second[...] = own_second
    hi = own_first.astype(BF16)
    low = (own_first - hi.astype(F32)).astype(BF16)
    joined[0:768, :] = fine_first[...]
    joined[768:816, :] = own_first[:, 0:128]
    joined[816:864, :] = own_first[:, 128:256]
    f_before = bands[band, 48:96, :]
    total = mm_tn(f_before, hi) + mm_tn(f_before, low) + mm_tn(bands[band, 0:48, :], own_second)
    packed[:, 0:8, :] = total[:, 0:128].reshape(N_PLANE, 8, 128)
    packed[:, 8:16, :] = total[:, 128:256].reshape(N_PLANE, 8, 128)
    for chunk in range(N_PLANE):
        packed[chunk, 16:20, :] = fine_partial[4 * chunk : 4 * chunk + 4, :]
    send[...] = packed[...][:, 0:20, :].astype(BF16)


def sum_body(parts, out):
    total = parts[0].astype(F32)
    for source in range(1, parts.shape[0]):
        total = total + parts[source].astype(F32)
    rounded = total.astype(BF16)
    for target in range(out.shape[0]):
        out[target] = rounded


def unpack_body(parts, coarse, fine):
    values = parts[...].astype(F32) * (1.0 / N_FRAMES)
    coarse[:, 0:128] = values[:, 0:8, :].reshape(256, 128)
    coarse[:, 128:256] = values[:, 8:16, :].reshape(256, 128)
    for chunk in range(N_PLANE):
        fine[4 * chunk : 4 * chunk + 4, :] = values[chunk, 16:20, :]


def finish_body(returned, middle, from_above, from_below, weight, coarse_second, coarse_weight, fine_out, coarse_out):
    w = weight[...]
    total = returned[0:768, :] + middle[...].astype(F32)
    top = (total[0:384, :] + from_above[...].astype(F32)).astype(BF16)
    bottom = (total[384:768, :] + from_below[...].astype(F32)).astype(BF16)
    fine_out[0:384, :] = mm_nt(top, w).astype(BF16)
    fine_out[384:768, :] = mm_nt(bottom, w).astype(BF16)
    w = coarse_weight[...]
    second = coarse_second[...].astype(F32)
    left = (returned[768:816, :] + second[:, 0:128]).astype(BF16)
    right = (returned[816:864, :] + second[:, 128:256]).astype(BF16)
    coarse_out[...] = (mm_nt(left, w[:, 0:128]) + mm_nt(right, w[:, 128:256])).astype(BF16)


def shifted(value, frames, rows):
    pairs = [
        (f * N_ROWS + r, (f + frames) % N_FRAMES * N_ROWS + r + rows)
        for f in range(N_FRAMES)
        for r in range(max(0, -rows), min(N_ROWS, N_ROWS - rows))
    ]
    return lax.ppermute(value, ALL, pairs)


def local(coarse_features, fine_features, coarse_weight, fine_weight, grad_refined, grad_back):
    coarse_own = coarse_features.reshape(48, 256)
    fine_own = fine_features.reshape(768, 128)
    taken = call(
        prepare_body,
        shape(928, 128),
        [
            pltpu.VMEM((64, 128), F32),
            pltpu.VMEM((48, 256), BF16),
            pltpu.VMEM((2, 768), F32),
            pltpu.VMEM((2, 48), F32),
            pltpu.SemaphoreType.DMA((4,)),
        ],
        n_in=4, flops=10**9, nbytes=10**6, kind=HBM, room=60,
    )(coarse_own, fine_own, grad_refined.reshape(2, 768), grad_back.reshape(2, 48))
    taken, rims = lax.optimization_barrier((taken, fine_own))
    taken = shifted(taken, 1, 0)
    above = shifted(rims[384:768], 0, 1)
    below = shifted(rims[0:384], 0, -1)
    outgoing = call(pack_body, shape(N_ROWS, 112, 256), n_in=2, nbytes=10**6)(coarse_own, taken)
    bands = lax.all_to_all(outgoing, ROWS, 0, 0, tiled=True)
    fine_first, middle, up_out, down_out, fine_partial = call(
        fine_body,
        (shape(768, 128, dtype=F32), shape(768, 128), shape(384, 128), shape(384, 128), shape(128, 128, dtype=F32)),
        [
            pltpu.VMEM((8, 96, 128), F32),
            pltpu.VMEM((8, 96, 128), BF16),
            pltpu.VMEM((16, 128, 128), BF16),
            pltpu.VMEM((16, 128, 128), F32),
            pltpu.VMEM((8, 768), F32),
            pltpu.VMEM((12, 64, 128), F32),
        ],
        n_in=5, flops=20 * 10**9, nbytes=4 * 10**6,
    )(taken, fine_own, above, below, fine_weight)
    back_up = shifted(up_out, 0, -1)
    back_down = shifted(down_out, 0, 1)
    coarse_second, joined, send = call(
        coarse_body,
        (shape(48, 256), shape(864, 128, dtype=F32), shape(N_PLANE, 20, 128)),
        [
            pltpu.VMEM((384, 256), F32),
            pltpu.VMEM((384, 256), F32),
            pltpu.VMEM((N_PLANE, 24, 128), F32),
        ],
        n_in=4, flops=3 * 10**9, nbytes=2 * 10**6,
    )(bands, coarse_weight, fine_partial, fine_first)
    returned = shifted(joined, -1, 0)
    parts = lax.all_to_all(send, PLANE, 0, 0, tiled=True)
    copies = call(sum_body, shape(N_Z, 20, 128), n_in=1, nbytes=10**6)(parts)
    parts = lax.all_to_all(copies, "z", 0, 0, axis_index_groups=[[(9 + i) % N_Z for i in range(N_Z)]], tiled=True)
    copies = call(sum_body, shape(N_PLANE, 20, 128), n_in=1, nbytes=10**6)(parts)
    parts = lax.all_to_all(copies, PLANE, 0, 0, tiled=True)
    coarse_total, fine_total = call(
        unpack_body, (shape(256, 256, dtype=F32), shape(128, 128, dtype=F32)), n_in=1, nbytes=10**6
    )(parts)
    fine_grad, coarse_grad = call(
        finish_body, (shape(768, 128), shape(48, 256)), n_in=7, flops=20 * 10**9, nbytes=10**6
    )(returned, middle, back_down, back_up, fine_weight, coarse_second, coarse_weight)
    return (
        coarse_grad.reshape(coarse_features.shape),
        fine_grad.reshape(fine_features.shape),
        coarse_total,
        fine_total,
    )


def solution(mesh):
    fine_mesh = Mesh(mesh.devices.reshape(16, 2, 2, 4, 2), ALL)
    in_specs = (
        P(FRAMES, ROWS, None, None),
        P(FRAMES, ROWS, None, None),
        P(),
        P(),
        P(FRAMES, None, ROWS),
        P(FRAMES, None, ROWS),
    )
    out_specs = (P(FRAMES, ROWS, None, None), P(FRAMES, ROWS, None, None), P(), P())
    return jax.shard_map(local, mesh=fine_mesh, in_specs=in_specs, out_specs=out_specs, check_vma=False)
```

```python
import math

import jax
import jax.numpy as jnp
from jax import lax
from jax.experimental import pallas as pl
from jax.experimental.pallas import tpu as pltpu
from jax.sharding import Mesh, PartitionSpec as P

F32 = jnp.float32
BF16 = jnp.bfloat16
FRAMES = ("z", "yh", "core")
ROWS = ("x", "yl")
PLANE = ("yh", "core", "x", "yl")
ALL = FRAMES + ROWS
N_FRAMES, N_ROWS, N_PLANE, N_Z = 64, 8, 32, 16
VMEM = pl.BlockSpec(memory_space=pltpu.VMEM)
HBM = pl.BlockSpec(memory_space=pltpu.HBM)


def call(body, outs, scratch=(), n_in=0, flops=0, nbytes=0, kind=VMEM, room=40):
    return pl.pallas_call(
        body,
        out_shape=outs,
        in_specs=[kind] * n_in,
        out_specs=jax.tree.map(lambda _: VMEM, outs),
        scratch_shapes=list(scratch),
        compiler_params=pltpu.CompilerParams(vmem_limit_bytes=room * 1024 * 1024),
        cost_estimate=pl.CostEstimate(flops=flops, bytes_accessed=nbytes, transcendentals=0),
    )


def shape(*dims, dtype=BF16):
    return jax.ShapeDtypeStruct(dims, dtype)


def mm(a, b):
    return lax.dot_general(a, b, (((1,), (0,)), ((), ())), preferred_element_type=F32)


def mm_nt(a, b):
    return lax.dot_general(a, b, (((1,), (1,)), ((), ())), preferred_element_type=F32)


def mm_tn(a, b):
    return lax.dot_general(a, b, (((0,), (0,)), ((), ())), preferred_element_type=F32)


def split3(value):
    hi = value.astype(BF16)
    rest = value - hi.astype(F32)
    mid = rest.astype(BF16)
    low = (rest - mid.astype(F32)).astype(BF16)
    return hi, mid, low


def iota(dims, axis):
    return lax.broadcasted_iota(jnp.int32, dims, axis)


def key_frame_present():
    frame = (lax.axis_index("z") * 2 + lax.axis_index("yh")) * 2 + lax.axis_index("core")
    return jnp.minimum(frame, 1).astype(F32)


def prepare_body(coarse_hbm, fine_hbm, refined_hbm, back_hbm, taken, cots, coarse, refined, back, sems):
    copies = [
        pltpu.make_async_copy(refined_hbm, refined, sems.at[0]),
        pltpu.make_async_copy(back_hbm, back, sems.at[1]),
        pltpu.make_async_copy(coarse_hbm, coarse, sems.at[2]),
        pltpu.make_async_copy(fine_hbm, taken.at[pl.ds(0, 768), :], sems.at[3]),
    ]
    for copy in copies:
        copy.start()
    cell = iota((768, 128), 0)
    low = (cell >= 384).astype(jnp.int32)
    cell = cell - 384 * low
    line = (cell >= 96).astype(jnp.int32) + (cell >= 192).astype(jnp.int32) + (cell >= 288).astype(jnp.int32)
    column = lax.shift_right_logical(cell - 96 * line, 2)
    pool = (iota((768, 128), 1) == column + 24 * low).astype(F32).astype(BF16)
    cots[...] = jnp.zeros_like(cots)
    copies[0].wait()
    copies[1].wait()
    terms = split3(refined[...])
    for term in range(3):
        wide = terms[term].astype(F32)
        for k in range(6):
            at = 16 * term + 2 * k
            cots[at : at + 2, :] = wide[:, 128 * k : 128 * k + 128]
    cots[48:50, :] = 4.0 * (mm(terms[0], pool) + (mm(terms[1], pool) + mm(terms[2], pool)))
    cots[50:52, 0:48] = back[...]
    hi, mid, rest = split3(cots[48:52, :])
    cots[48:52, :] = hi.astype(F32)
    cots[52:56, :] = mid.astype(F32)
    cots[56:60, :] = rest.astype(F32)
    taken[864:928, :] = cots[...].astype(BF16)
    copies[2].wait()
    taken[768:816, :] = coarse[:, 0:128]
    taken[816:864, :] = coarse[:, 128:256]
    copies[3].wait()


def pack_body(coarse, taken, weight, out):
    w = weight[...]
    own = (mm(coarse[...], w) * key_frame_present()).astype(BF16)
    before = (mm(taken[768:816, :], w[0:128, :]) + mm(taken[816:864, :], w[128:256, :])).astype(BF16)
    cots = jnp.concatenate([taken[912:928, :], jnp.zeros((16, 128), BF16)], axis=1)
    for band in range(N_ROWS):
        out[band, 0:48, :] = own
        out[band, 48:96, :] = before
        out[band, 96:112, :] = cots


def fine_body(taken, own, above, below, weight, first_out, mid_out, up_out, down_out, partial,
              first, queries, keys, key_grad, turned, window):
    scale = 1.0 / math.sqrt(128.0)
    w = weight[...]
    present = key_frame_present()
    queries[...] = mm(taken[0:768, :], w).astype(BF16).reshape(8, 96, 128)
    keys[:, 0:16, :] = jnp.zeros((16, 16, 128), BF16)
    keys[:, 112:128, :] = jnp.zeros((16, 16, 128), BF16)
    keys[0:4, 16:112, :] = (mm(above[...], w) * present).astype(BF16).reshape(4, 96, 128)
    keys[4:12, 16:112, :] = (mm(own[...], w) * present).astype(BF16).reshape(8, 96, 128)
    keys[12:16, 16:112, :] = (mm(below[...], w) * present).astype(BF16).reshape(4, 96, 128)
    key_grad[...] = jnp.zeros_like(key_grad)
    turned[...] = jnp.zeros_like(turned)
    terms = taken[864:912, :].astype(F32)
    refined = terms[0:16, :] + (terms[16:32, :] + terms[32:48, :])
    for k in range(6):
        turned[0:2, 128 * k : 128 * k + 128] = refined[2 * k : 2 * k + 2, :]
    upright = jnp.transpose(turned[...], (1, 0))
    lane = iota((1, 128), 1)
    query_x = jnp.bitwise_and(lane, 31).astype(F32)
    query_y = lax.shift_right_logical(lane, 5).astype(F32)
    key_x = iota((64, 128), 0).astype(F32) - 16.0
    near_x = jnp.where(jnp.abs(key_x - query_x) < 4.5, 0.0, -1e30)
    for line in range(12):
        near_y = jnp.where(jnp.abs(line - 4.0 - query_y) < 4.5, 0.0, -1e30)
        window[line] = jnp.minimum(near_x, near_y)
    for part in range(2):
        for column in range(3):
            q = queries[4 * part : 4 * part + 4, 32 * column : 32 * column + 32, :].reshape(128, 128)
            k = keys[4 * part : 4 * part + 12, 32 * column : 32 * column + 64, :].reshape(768, 128)
            pieces = [(4 * part + line) * 96 + 32 * column for line in range(4)]
            cot = jnp.transpose(jnp.concatenate([upright[at : at + 32, :] for at in pieces], axis=0), (1, 0))
            gx, gy = cot[0:1, :], cot[1:2, :]
            s = mm_nt(k, q).reshape(12, 64, 128) + window[...]
            top = jnp.max(jnp.max(s, axis=0), axis=0, keepdims=True)
            e = jnp.exp2((s - top) * (scale * math.log2(math.e)))
            by_x = jnp.sum(e, axis=0)
            inverse = 1.0 / jnp.sum(by_x, axis=0, keepdims=True)
            mean_x = jnp.sum(by_x * key_x, axis=0, keepdims=True) * inverse
            mean_y = jnp.zeros((1, 128), F32)
            for line in range(12):
                mean_y = mean_y + (line - 4.0) * jnp.sum(e[line], axis=0, keepdims=True)
            mean_y = mean_y * inverse
            factor = inverse * scale
            gx, gy = gx * factor, gy * factor
            bend_x = gx * (key_x - mean_x)
            weights = jnp.concatenate(
                [(e[line] * (bend_x + gy * ((line - 4.0) - mean_y))).astype(BF16) for line in range(12)], axis=0
            )
            first[4 * part : 4 * part + 4, 32 * column : 32 * column + 32, :] = mm_tn(weights, k).reshape(4, 32, 128)
            key_grad[4 * part : 4 * part + 12, 32 * column : 32 * column + 64, :] += mm(weights, q).reshape(12, 64, 128)
    up_out[...] = (key_grad[0:4, 16:112, :] * present).astype(BF16).reshape(384, 128)
    mid_out[...] = (key_grad[4:12, 16:112, :] * present).astype(BF16).reshape(768, 128)
    down_out[...] = (key_grad[12:16, 16:112, :] * present).astype(BF16).reshape(384, 128)
    exact = first[...].reshape(768, 128)
    hi = exact.astype(BF16)
    low = (exact - hi.astype(F32)).astype(BF16)
    first_out[...] = exact
    total = mm_tn(taken[0:768, :], hi) + mm_tn(taken[0:768, :], low)
    total = total + mm_tn(own[...], mid_out[...])
    partial[...] = total + mm_tn(above[...], up_out[...]) + mm_tn(below[...], down_out[...])


def match(scores, cot_x, cot_y):
    e = jnp.exp2((scores - jnp.max(scores, axis=0, keepdims=True)) * (math.log2(math.e) / 16.0)).reshape(16, 24, 384)
    by_x = jnp.sum(e, axis=0)
    inverse = 1.0 / jnp.sum(by_x, axis=0, keepdims=True)
    key_x = iota((24, 384), 0).astype(F32)
    mean_x = jnp.sum(by_x * key_x, axis=0, keepdims=True) * inverse
    mean_y = jnp.zeros((1, 384), F32)
    for line in range(1, 16):
        mean_y = mean_y + float(line) * jnp.sum(e[line], axis=0, keepdims=True)
    mean_y = mean_y * inverse
    factor = inverse * (1.0 / 16.0)
    cot_x, cot_y = cot_x * factor, cot_y * factor
    bend_x = cot_x * (key_x - mean_x)
    lines = [e[line] * (bend_x + cot_y * (float(line) - mean_y)) for line in range(16)]
    return jnp.concatenate(lines, axis=0).astype(BF16)


def coarse_body(bands, coarse, taken, fine_partial, fine_first, second, joined, send,
                sums_first, sums_second, packed):
    band, present = lax.axis_index("x") * 2 + lax.axis_index("yl"), key_frame_present()
    qa = bands[:, 48:96, :].reshape(384, 256)
    qb = bands[:, 0:48, :].reshape(384, 256)
    flat = jnp.zeros((16, 384), F32)
    ahead = iota((128, 384), 1) - iota((128, 384), 0)
    for source in range(N_ROWS):
        place = (ahead == 48 * source).astype(F32).astype(BF16)
        flat = flat + mm(bands[source, 96:112, 0:128], place)
    cots = flat[0:4, :] + (flat[4:8, :] + flat[8:12, :])
    forward_t = match(mm_nt(qb, qa), cots[0:1, :], cots[1:2, :])
    backward_t = match(mm_nt(qa, qb), cots[2:3, :], cots[3:4, :])
    sums_first[...] = mm_tn(forward_t, qb) + mm(backward_t, qb)
    sums_second[...] = mm(forward_t, qa) + mm_tn(backward_t, qa)
    mine = pl.ds(pl.multiple_of(band * 48, 16), 48)
    own_first = sums_first[mine, :]
    own_second = (sums_second[mine, :] * present).astype(BF16)
    second[...] = own_second
    hi = own_first.astype(BF16)
    low = (own_first - hi.astype(F32)).astype(BF16)
    joined[0:768, :] = fine_first[...]
    joined[768:816, :] = own_first[:, 0:128]
    joined[816:864, :] = own_first[:, 128:256]
    f_before = jnp.concatenate([taken[768:816, :], taken[816:864, :]], axis=1)
    total = mm_tn(f_before, hi) + mm_tn(f_before, low) + mm_tn(coarse[...], own_second)
    packed[:, 0:8, :] = total[:, 0:128].reshape(N_PLANE, 8, 128)
    packed[:, 8:16, :] = total[:, 128:256].reshape(N_PLANE, 8, 128)
    for chunk in range(N_PLANE):
        packed[chunk, 16:20, :] = fine_partial[4 * chunk : 4 * chunk + 4, :]
    send[...] = packed[...][:, 0:20, :].astype(BF16)


def sum_body(parts, out):
    total = parts[0].astype(F32)
    for source in range(1, parts.shape[0]):
        total = total + parts[source].astype(F32)
    rounded = total.astype(BF16)
    for target in range(out.shape[0]):
        out[target] = rounded


def unpack_body(parts, coarse, fine):
    values = parts[...].astype(F32) * (1.0 / N_FRAMES)
    coarse[:, 0:128] = values[:, 0:8, :].reshape(256, 128)
    coarse[:, 128:256] = values[:, 8:16, :].reshape(256, 128)
    for chunk in range(N_PLANE):
        fine[4 * chunk : 4 * chunk + 4, :] = values[chunk, 16:20, :]


def finish_body(returned, middle, from_above, from_below, weight, coarse_second, coarse_weight, fine_out, coarse_out):
    w = weight[...]
    total = returned[0:768, :] + middle[...].astype(F32)
    top = (total[0:384, :] + from_above[...].astype(F32)).astype(BF16)
    bottom = (total[384:768, :] + from_below[...].astype(F32)).astype(BF16)
    fine_out[0:384, :] = mm_nt(top, w).astype(BF16)
    fine_out[384:768, :] = mm_nt(bottom, w).astype(BF16)
    w = coarse_weight[...]
    second = coarse_second[...].astype(F32)
    left = (returned[768:816, :] + second[:, 0:128]).astype(BF16)
    right = (returned[816:864, :] + second[:, 128:256]).astype(BF16)
    coarse_out[...] = (mm_nt(left, w[:, 0:128]) + mm_nt(right, w[:, 128:256])).astype(BF16)


def shifted(value, frames, rows):
    pairs = [
        (f * N_ROWS + r, (f + frames) % N_FRAMES * N_ROWS + r + rows)
        for f in range(N_FRAMES)
        for r in range(max(0, -rows), min(N_ROWS, N_ROWS - rows))
    ]
    return lax.ppermute(value, ALL, pairs)


def local(coarse_features, fine_features, coarse_weight, fine_weight, grad_refined, grad_back):
    coarse_own = coarse_features.reshape(48, 256)
    fine_own = fine_features.reshape(768, 128)
    taken = call(
        prepare_body,
        shape(928, 128),
        [
            pltpu.VMEM((64, 128), F32),
            pltpu.VMEM((48, 256), BF16),
            pltpu.VMEM((2, 768), F32),
            pltpu.VMEM((2, 48), F32),
            pltpu.SemaphoreType.DMA((4,)),
        ],
        n_in=4, flops=10**9, nbytes=10**6, kind=HBM, room=60,
    )(coarse_own, fine_own, grad_refined.reshape(2, 768), grad_back.reshape(2, 48))
    taken, rims = lax.optimization_barrier((taken, fine_own))
    taken = shifted(taken, 1, 0)
    above = shifted(rims[384:768], 0, 1)
    below = shifted(rims[0:384], 0, -1)
    outgoing = call(pack_body, shape(N_ROWS, 112, 256), n_in=3, nbytes=10**6)(coarse_own, taken, coarse_weight)
    bands = lax.all_to_all(outgoing, ROWS, 0, 0, tiled=True)
    fine_first, middle, up_out, down_out, fine_partial = call(
        fine_body,
        (shape(768, 128, dtype=F32), shape(768, 128), shape(384, 128), shape(384, 128), shape(128, 128, dtype=F32)),
        [
            pltpu.VMEM((8, 96, 128), F32),
            pltpu.VMEM((8, 96, 128), BF16),
            pltpu.VMEM((16, 128, 128), BF16),
            pltpu.VMEM((16, 128, 128), F32),
            pltpu.VMEM((8, 768), F32),
            pltpu.VMEM((12, 64, 128), F32),
        ],
        n_in=5, flops=20 * 10**9, nbytes=4 * 10**6,
    )(taken, fine_own, above, below, fine_weight)
    back_up = shifted(up_out, 0, -1)
    back_down = shifted(down_out, 0, 1)
    coarse_second, joined, send = call(
        coarse_body,
        (shape(48, 256), shape(864, 128, dtype=F32), shape(N_PLANE, 20, 128)),
        [
            pltpu.VMEM((384, 256), F32),
            pltpu.VMEM((384, 256), F32),
            pltpu.VMEM((N_PLANE, 24, 128), F32),
        ],
        n_in=5, flops=3 * 10**9, nbytes=2 * 10**6,
    )(bands, coarse_own, taken, fine_partial, fine_first)
    returned = shifted(joined, -1, 0)
    parts = lax.all_to_all(send, PLANE, 0, 0, tiled=True)
    copies = call(sum_body, shape(N_Z, 20, 128), n_in=1, nbytes=10**6)(parts)
    parts = lax.all_to_all(copies, "z", 0, 0, axis_index_groups=[[(9 + i) % N_Z for i in range(N_Z)]], tiled=True)
    copies = call(sum_body, shape(N_PLANE, 20, 128), n_in=1, nbytes=10**6)(parts)
    parts = lax.all_to_all(copies, PLANE, 0, 0, tiled=True)
    coarse_total, fine_total = call(
        unpack_body, (shape(256, 256, dtype=F32), shape(128, 128, dtype=F32)), n_in=1, nbytes=10**6
    )(parts)
    fine_grad, coarse_grad = call(
        finish_body, (shape(768, 128), shape(48, 256)), n_in=7, flops=20 * 10**9, nbytes=10**6
    )(returned, middle, back_down, back_up, fine_weight, coarse_second, coarse_weight)
    return (
        coarse_grad.reshape(coarse_features.shape),
        fine_grad.reshape(fine_features.shape),
        coarse_total,
        fine_total,
    )


def solution(mesh):
    fine_mesh = Mesh(mesh.devices.reshape(16, 2, 2, 4, 2), ALL)
    in_specs = (
        P(FRAMES, ROWS, None, None),
        P(FRAMES, ROWS, None, None),
        P(),
        P(),
        P(FRAMES, None, ROWS),
        P(FRAMES, None, ROWS),
    )
    out_specs = (P(FRAMES, ROWS, None, None), P(FRAMES, ROWS, None, None), P(), P())
    return jax.shard_map(local, mesh=fine_mesh, in_specs=in_specs, out_specs=out_specs, check_vma=False)
```

```python
import math

import jax
import jax.numpy as jnp
from jax import lax
from jax.experimental import pallas as pl
from jax.experimental.pallas import tpu as pltpu
from jax.sharding import Mesh, PartitionSpec as P

F32 = jnp.float32
BF16 = jnp.bfloat16
FRAMES = ("z", "yh", "core")
ROWS = ("x", "yl")
PLANE = ("yh", "core", "x", "yl")
ALL = FRAMES + ROWS
N_FRAMES, N_ROWS, N_PLANE, N_Z = 64, 8, 32, 16
VMEM = pl.BlockSpec(memory_space=pltpu.VMEM)
HBM = pl.BlockSpec(memory_space=pltpu.HBM)


def call(body, outs, scratch=(), n_in=0, flops=0, nbytes=0, kind=VMEM, room=40):
    return pl.pallas_call(
        body,
        out_shape=outs,
        in_specs=[kind] * n_in,
        out_specs=jax.tree.map(lambda _: VMEM, outs),
        scratch_shapes=list(scratch),
        compiler_params=pltpu.CompilerParams(vmem_limit_bytes=room * 1024 * 1024),
        cost_estimate=pl.CostEstimate(flops=flops, bytes_accessed=nbytes, transcendentals=0),
    )


def shape(*dims, dtype=BF16):
    return jax.ShapeDtypeStruct(dims, dtype)


def mm(a, b):
    return lax.dot_general(a, b, (((1,), (0,)), ((), ())), preferred_element_type=F32)


def mm_nt(a, b):
    return lax.dot_general(a, b, (((1,), (1,)), ((), ())), preferred_element_type=F32)


def mm_tn(a, b):
    return lax.dot_general(a, b, (((0,), (0,)), ((), ())), preferred_element_type=F32)


def split3(value):
    hi = value.astype(BF16)
    rest = value - hi.astype(F32)
    mid = rest.astype(BF16)
    low = (rest - mid.astype(F32)).astype(BF16)
    return hi, mid, low


def iota(dims, axis):
    return lax.broadcasted_iota(jnp.int32, dims, axis)


def key_frame_present():
    frame = (lax.axis_index("z") * 2 + lax.axis_index("yh")) * 2 + lax.axis_index("core")
    return jnp.minimum(frame, 1).astype(F32)


def prepare_body(coarse_hbm, fine_hbm, refined_hbm, back_hbm, taken, cots, coarse, refined, back, sems):
    copies = [
        pltpu.make_async_copy(refined_hbm, refined, sems.at[0]),
        pltpu.make_async_copy(back_hbm, back, sems.at[1]),
        pltpu.make_async_copy(coarse_hbm, coarse, sems.at[2]),
        pltpu.make_async_copy(fine_hbm, taken.at[pl.ds(0, 768), :], sems.at[3]),
    ]
    for copy in copies:
        copy.start()
    cell = iota((768, 128), 0)
    low = (cell >= 384).astype(jnp.int32)
    cell = cell - 384 * low
    line = (cell >= 96).astype(jnp.int32) + (cell >= 192).astype(jnp.int32) + (cell >= 288).astype(jnp.int32)
    column = lax.shift_right_logical(cell - 96 * line, 2)
    pool = (iota((768, 128), 1) == column + 24 * low).astype(F32).astype(BF16)
    cots[...] = jnp.zeros_like(cots)
    copies[0].wait()
    copies[1].wait()
    terms = split3(refined[...])
    for term in range(3):
        wide = terms[term].astype(F32)
        for k in range(6):
            at = 16 * term + 2 * k
            cots[at : at + 2, :] = wide[:, 128 * k : 128 * k + 128]
    cots[48:50, :] = 4.0 * (mm(terms[0], pool) + (mm(terms[1], pool) + mm(terms[2], pool)))
    cots[50:52, 0:48] = back[...]
    hi, mid, rest = split3(cots[48:52, :])
    cots[48:52, :] = hi.astype(F32)
    cots[52:56, :] = mid.astype(F32)
    cots[56:60, :] = rest.astype(F32)
    taken[864:928, :] = cots[...].astype(BF16)
    copies[2].wait()
    taken[768:816, :] = coarse[:, 0:128]
    taken[816:864, :] = coarse[:, 128:256]
    copies[3].wait()


def pack_body(coarse, taken, weight, out):
    w = weight[...]
    own = (mm(coarse[...], w) * key_frame_present()).astype(BF16)
    before = (mm(taken[768:816, :], w[0:128, :]) + mm(taken[816:864, :], w[128:256, :])).astype(BF16)
    cots = jnp.concatenate([taken[912:928, :], jnp.zeros((16, 128), BF16)], axis=1)
    for band in range(N_ROWS):
        out[band, 0:48, :] = own
        out[band, 48:96, :] = before
        out[band, 96:112, :] = cots


def fine_body(taken, own, above, below, weight, first_out, mid_out, up_out, down_out, partial,
              first, queries, keys, key_grad, turned, window):
    scale = 1.0 / math.sqrt(128.0)
    w = weight[...]
    present = key_frame_present()
    queries[...] = mm(taken[0:768, :], w).astype(BF16).reshape(8, 96, 128)
    keys[:, 0:16, :] = jnp.zeros((16, 16, 128), BF16)
    keys[:, 112:128, :] = jnp.zeros((16, 16, 128), BF16)
    keys[0:4, 16:112, :] = (mm(above[...], w) * present).astype(BF16).reshape(4, 96, 128)
    keys[4:12, 16:112, :] = (mm(own[...], w) * present).astype(BF16).reshape(8, 96, 128)
    keys[12:16, 16:112, :] = (mm(below[...], w) * present).astype(BF16).reshape(4, 96, 128)
    key_grad[...] = jnp.zeros_like(key_grad)
    turned[...] = jnp.zeros_like(turned)
    terms = taken[864:912, :].astype(F32)
    refined = terms[0:16, :] + (terms[16:32, :] + terms[32:48, :])
    for k in range(6):
        turned[0:2, 128 * k : 128 * k + 128] = refined[2 * k : 2 * k + 2, :]
    upright = jnp.transpose(turned[...], (1, 0))
    lane = iota((1, 128), 1)
    query_x = jnp.bitwise_and(lane, 31).astype(F32)
    query_y = lax.shift_right_logical(lane, 5).astype(F32)
    key_x = iota((64, 128), 0).astype(F32) - 16.0
    near_x = jnp.where(jnp.abs(key_x - query_x) < 4.5, 0.0, -1e30)
    for line in range(12):
        near_y = jnp.where(jnp.abs(line - 4.0 - query_y) < 4.5, 0.0, -1e30)
        window[line] = jnp.minimum(near_x, near_y)
    for part in range(2):
        for column in range(3):
            q = queries[4 * part : 4 * part + 4, 32 * column : 32 * column + 32, :].reshape(128, 128)
            k = keys[4 * part : 4 * part + 12, 32 * column : 32 * column + 64, :].reshape(768, 128)
            pieces = [(4 * part + line) * 96 + 32 * column for line in range(4)]
            cot = jnp.transpose(jnp.concatenate([upright[at : at + 32, :] for at in pieces], axis=0), (1, 0))
            gx, gy = cot[0:1, :], cot[1:2, :]
            s = mm_nt(k, q).reshape(12, 64, 128) + window[...]
            top = jnp.max(jnp.max(s, axis=0), axis=0, keepdims=True)
            e = jnp.exp2((s - top) * (scale * math.log2(math.e)))
            by_x = jnp.sum(e, axis=0)
            inverse = 1.0 / jnp.sum(by_x, axis=0, keepdims=True)
            mean_x = jnp.sum(by_x * key_x, axis=0, keepdims=True) * inverse
            mean_y = jnp.zeros((1, 128), F32)
            for line in range(12):
                mean_y = mean_y + (line - 4.0) * jnp.sum(e[line], axis=0, keepdims=True)
            mean_y = mean_y * inverse
            factor = inverse * scale
            gx, gy = gx * factor, gy * factor
            bend_x = gx * (key_x - mean_x)
            weights = jnp.concatenate(
                [(e[line] * (bend_x + gy * ((line - 4.0) - mean_y))).astype(BF16) for line in range(12)], axis=0
            )
            first[4 * part : 4 * part + 4, 32 * column : 32 * column + 32, :] = mm_tn(weights, k).reshape(4, 32, 128)
            key_grad[4 * part : 4 * part + 12, 32 * column : 32 * column + 64, :] += mm(weights, q).reshape(12, 64, 128)
    up_out[...] = (key_grad[0:4, 16:112, :] * present).astype(BF16).reshape(384, 128)
    mid_out[...] = (key_grad[4:12, 16:112, :] * present).astype(BF16).reshape(768, 128)
    down_out[...] = (key_grad[12:16, 16:112, :] * present).astype(BF16).reshape(384, 128)
    exact = first[...].reshape(768, 128)
    hi = exact.astype(BF16)
    low = (exact - hi.astype(F32)).astype(BF16)
    first_out[...] = exact
    total = mm_tn(taken[0:768, :], hi) + mm_tn(taken[0:768, :], low)
    total = total + mm_tn(own[...], mid_out[...])
    partial[...] = total + mm_tn(above[...], up_out[...]) + mm_tn(below[...], down_out[...])


def match(scores, cot_x, cot_y):
    e = jnp.exp2((scores - jnp.max(scores, axis=0, keepdims=True)) * (math.log2(math.e) / 16.0)).reshape(16, 24, 384)
    by_x = jnp.sum(e, axis=0)
    inverse = 1.0 / jnp.sum(by_x, axis=0, keepdims=True)
    key_x = iota((24, 384), 0).astype(F32)
    mean_x = jnp.sum(by_x * key_x, axis=0, keepdims=True) * inverse
    mean_y = jnp.zeros((1, 384), F32)
    for line in range(1, 16):
        mean_y = mean_y + float(line) * jnp.sum(e[line], axis=0, keepdims=True)
    mean_y = mean_y * inverse
    factor = inverse * (1.0 / 16.0)
    cot_x, cot_y = cot_x * factor, cot_y * factor
    bend_x = cot_x * (key_x - mean_x)
    lines = [e[line] * (bend_x + cot_y * (float(line) - mean_y)) for line in range(16)]
    return jnp.concatenate(lines, axis=0).astype(BF16)


def coarse_body(bands, coarse, taken, fine_partial, fine_first, second, joined, send,
                sums_first, sums_second, packed):
    band, present = lax.axis_index("x") * 2 + lax.axis_index("yl"), key_frame_present()
    qa = bands[:, 48:96, :].reshape(384, 256)
    qb = bands[:, 0:48, :].reshape(384, 256)
    flat = jnp.zeros((16, 384), F32)
    ahead = iota((128, 384), 1) - iota((128, 384), 0)
    for source in range(N_ROWS):
        place = (ahead == 48 * source).astype(F32).astype(BF16)
        flat = flat + mm(bands[source, 96:112, 0:128], place)
    cots = flat[0:4, :] + (flat[4:8, :] + flat[8:12, :])
    forward_t = match(mm_nt(qb, qa), cots[0:1, :], cots[1:2, :])
    backward_t = match(mm_nt(qa, qb), cots[2:3, :], cots[3:4, :])
    sums_first[...] = mm_tn(forward_t, qb) + mm(backward_t, qb)
    sums_second[...] = mm(forward_t, qa) + mm_tn(backward_t, qa)
    mine = pl.ds(pl.multiple_of(band * 48, 16), 48)
    own_first = sums_first[mine, :]
    own_second = (sums_second[mine, :] * present).astype(BF16)
    second[...] = own_second
    hi = own_first.astype(BF16)
    low = (own_first - hi.astype(F32)).astype(BF16)
    joined[0:768, :] = fine_first[...]
    joined[768:816, :] = own_first[:, 0:128]
    joined[816:864, :] = own_first[:, 128:256]
    f_before = jnp.concatenate([taken[768:816, :], taken[816:864, :]], axis=1)
    total = mm_tn(f_before, hi) + mm_tn(f_before, low) + mm_tn(coarse[...], own_second)
    packed[:, 0:8, :] = total[:, 0:128].reshape(N_PLANE, 8, 128)
    packed[:, 8:16, :] = total[:, 128:256].reshape(N_PLANE, 8, 128)
    for chunk in range(N_PLANE):
        packed[chunk, 16:20, :] = fine_partial[4 * chunk : 4 * chunk + 4, :]
    send[...] = packed[...][:, 0:20, :].astype(BF16)


def sum_body(parts, out):
    total = parts[0].astype(F32)
    for source in range(1, parts.shape[0]):
        total = total + parts[source].astype(F32)
    rounded = total.astype(BF16)
    for target in range(out.shape[0]):
        out[target] = rounded


def unpack_body(parts, coarse, fine):
    values = parts[...].astype(F32) * (1.0 / N_FRAMES)
    coarse[:, 0:128] = values[:, 0:8, :].reshape(256, 128)
    coarse[:, 128:256] = values[:, 8:16, :].reshape(256, 128)
    for chunk in range(N_PLANE):
        fine[4 * chunk : 4 * chunk + 4, :] = values[chunk, 16:20, :]


def finish_body(returned, middle, from_above, from_below, weight, coarse_second, coarse_weight, fine_out, coarse_out):
    w = weight[...]
    total = returned[0:768, :] + middle[...].astype(F32)
    top = (total[0:384, :] + from_above[...].astype(F32)).astype(BF16)
    bottom = (total[384:768, :] + from_below[...].astype(F32)).astype(BF16)
    fine_out[0:384, :] = mm_nt(top, w).astype(BF16)
    fine_out[384:768, :] = mm_nt(bottom, w).astype(BF16)
    w = coarse_weight[...]
    second = coarse_second[...].astype(F32)
    left = (returned[768:816, :] + second[:, 0:128]).astype(BF16)
    right = (returned[816:864, :] + second[:, 128:256]).astype(BF16)
    coarse_out[...] = (mm_nt(left, w[:, 0:128]) + mm_nt(right, w[:, 128:256])).astype(BF16)


def shifted(value, frames, rows):
    pairs = [
        (f * N_ROWS + r, (f + frames) % N_FRAMES * N_ROWS + r + rows)
        for f in range(N_FRAMES)
        for r in range(max(0, -rows), min(N_ROWS, N_ROWS - rows))
    ]
    return lax.ppermute(value, ALL, pairs)


def local(coarse_features, fine_features, coarse_weight, fine_weight, grad_refined, grad_back):
    coarse_own = coarse_features.reshape(48, 256)
    fine_own = fine_features.reshape(768, 128)
    taken = call(
        prepare_body,
        shape(928, 128),
        [
            pltpu.VMEM((64, 128), F32),
            pltpu.VMEM((48, 256), BF16),
            pltpu.VMEM((2, 768), F32),
            pltpu.VMEM((2, 48), F32),
            pltpu.SemaphoreType.DMA((4,)),
        ],
        n_in=4, flops=10**9, nbytes=10**6, kind=HBM, room=60,
    )(coarse_own, fine_own, grad_refined.reshape(2, 768), grad_back.reshape(2, 48))
    rims = fine_own
    taken = shifted(taken, 1, 0)
    above = shifted(rims[384:768], 0, 1)
    below = shifted(rims[0:384], 0, -1)
    outgoing = call(pack_body, shape(N_ROWS, 112, 256), n_in=3, nbytes=10**6)(coarse_own, taken, coarse_weight)
    bands = lax.all_to_all(outgoing, ROWS, 0, 0, tiled=True)
    fine_first, middle, up_out, down_out, fine_partial = call(
        fine_body,
        (shape(768, 128, dtype=F32), shape(768, 128), shape(384, 128), shape(384, 128), shape(128, 128, dtype=F32)),
        [
            pltpu.VMEM((8, 96, 128), F32),
            pltpu.VMEM((8, 96, 128), BF16),
            pltpu.VMEM((16, 128, 128), BF16),
            pltpu.VMEM((16, 128, 128), F32),
            pltpu.VMEM((8, 768), F32),
            pltpu.VMEM((12, 64, 128), F32),
        ],
        n_in=5, flops=20 * 10**9, nbytes=4 * 10**6,
    )(taken, fine_own, above, below, fine_weight)
    back_up = shifted(up_out, 0, -1)
    back_down = shifted(down_out, 0, 1)
    coarse_second, joined, send = call(
        coarse_body,
        (shape(48, 256), shape(864, 128, dtype=F32), shape(N_PLANE, 20, 128)),
        [
            pltpu.VMEM((384, 256), F32),
            pltpu.VMEM((384, 256), F32),
            pltpu.VMEM((N_PLANE, 24, 128), F32),
        ],
        n_in=5, flops=3 * 10**9, nbytes=2 * 10**6,
    )(bands, coarse_own, taken, fine_partial, fine_first)
    returned = shifted(joined, -1, 0)
    parts = lax.all_to_all(send, PLANE, 0, 0, axis_index_groups=[[(20 + i) % N_PLANE for i in range(N_PLANE)]], tiled=True)
    copies = call(sum_body, shape(N_Z, 20, 128), n_in=1, nbytes=10**6)(parts)
    parts = lax.all_to_all(copies, "z", 0, 0, axis_index_groups=[[(9 + i) % N_Z for i in range(N_Z)]], tiled=True)
    copies = call(sum_body, shape(N_PLANE, 20, 128), n_in=1, nbytes=10**6)(parts)
    parts = lax.all_to_all(copies, PLANE, 0, 0, axis_index_groups=[[(20 + i) % N_PLANE for i in range(N_PLANE)]], tiled=True)
    coarse_total, fine_total = call(
        unpack_body, (shape(256, 256, dtype=F32), shape(128, 128, dtype=F32)), n_in=1, nbytes=10**6
    )(parts)
    fine_grad, coarse_grad = call(
        finish_body, (shape(768, 128), shape(48, 256)), n_in=7, flops=20 * 10**9, nbytes=10**6
    )(returned, middle, back_down, back_up, fine_weight, coarse_second, coarse_weight)
    return (
        coarse_grad.reshape(coarse_features.shape),
        fine_grad.reshape(fine_features.shape),
        coarse_total,
        fine_total,
    )


def solution(mesh):
    fine_mesh = Mesh(mesh.devices.reshape(16, 2, 2, 4, 2), ALL)
    in_specs = (
        P(FRAMES, ROWS, None, None),
        P(FRAMES, ROWS, None, None),
        P(),
        P(),
        P(FRAMES, None, ROWS),
        P(FRAMES, None, ROWS),
    )
    out_specs = (P(FRAMES, ROWS, None, None), P(FRAMES, ROWS, None, None), P(), P())
    return jax.shard_map(local, mesh=fine_mesh, in_specs=in_specs, out_specs=out_specs, check_vma=False)
```

```python
import math

import jax
import jax.numpy as jnp
from jax import lax
from jax.experimental import pallas as pl
from jax.experimental.pallas import tpu as pltpu
from jax.sharding import Mesh, PartitionSpec as P

F32 = jnp.float32
BF16 = jnp.bfloat16
FRAMES = ("z", "yh", "core")
ROWS = ("x", "yl")
PLANE = ("yh", "core", "x", "yl")
ALL = FRAMES + ROWS
N_FRAMES, N_ROWS, N_PLANE, N_Z = 64, 8, 32, 16
VMEM = pl.BlockSpec(memory_space=pltpu.VMEM)
HBM = pl.BlockSpec(memory_space=pltpu.HBM)


def call(body, outs, scratch=(), n_in=0, flops=0, nbytes=0, kind=VMEM, room=40):
    return pl.pallas_call(
        body,
        out_shape=outs,
        in_specs=[kind] * n_in,
        out_specs=jax.tree.map(lambda _: VMEM, outs),
        scratch_shapes=list(scratch),
        compiler_params=pltpu.CompilerParams(vmem_limit_bytes=room * 1024 * 1024),
        cost_estimate=pl.CostEstimate(flops=flops, bytes_accessed=nbytes, transcendentals=0),
    )


def shape(*dims, dtype=BF16):
    return jax.ShapeDtypeStruct(dims, dtype)


def mm(a, b):
    return lax.dot_general(a, b, (((1,), (0,)), ((), ())), preferred_element_type=F32)


def mm_nt(a, b):
    return lax.dot_general(a, b, (((1,), (1,)), ((), ())), preferred_element_type=F32)


def mm_tn(a, b):
    return lax.dot_general(a, b, (((0,), (0,)), ((), ())), preferred_element_type=F32)


def split3(value):
    hi = value.astype(BF16)
    rest = value - hi.astype(F32)
    mid = rest.astype(BF16)
    low = (rest - mid.astype(F32)).astype(BF16)
    return hi, mid, low


def iota(dims, axis):
    return lax.broadcasted_iota(jnp.int32, dims, axis)


def key_frame_present():
    frame = (lax.axis_index("z") * 2 + lax.axis_index("yh")) * 2 + lax.axis_index("core")
    return jnp.minimum(frame, 1).astype(F32)


def prepare_body(coarse_hbm, fine_hbm, refined_hbm, back_hbm, taken, cots, coarse, refined, back, sems):
    copies = [
        pltpu.make_async_copy(refined_hbm, refined, sems.at[0]),
        pltpu.make_async_copy(back_hbm, back, sems.at[1]),
        pltpu.make_async_copy(coarse_hbm, coarse, sems.at[2]),
        pltpu.make_async_copy(fine_hbm, taken.at[pl.ds(0, 768), :], sems.at[3]),
    ]
    for copy in copies:
        copy.start()
    cell = iota((768, 128), 0)
    low = (cell >= 384).astype(jnp.int32)
    cell = cell - 384 * low
    line = (cell >= 96).astype(jnp.int32) + (cell >= 192).astype(jnp.int32) + (cell >= 288).astype(jnp.int32)
    column = lax.shift_right_logical(cell - 96 * line, 2)
    pool = (iota((768, 128), 1) == column + 24 * low).astype(F32).astype(BF16)
    cots[...] = jnp.zeros_like(cots)
    copies[0].wait()
    copies[1].wait()
    terms = split3(refined[...])
    for term in range(3):
        wide = terms[term].astype(F32)
        for k in range(6):
            at = 16 * term + 2 * k
            cots[at : at + 2, :] = wide[:, 128 * k : 128 * k + 128]
    cots[48:50, :] = 4.0 * (mm(terms[0], pool) + (mm(terms[1], pool) + mm(terms[2], pool)))
    cots[50:52, 0:48] = back[...]
    hi, mid, rest = split3(cots[48:52, :])
    cots[48:52, :] = hi.astype(F32)
    cots[52:56, :] = mid.astype(F32)
    cots[56:60, :] = rest.astype(F32)
    taken[864:928, :] = cots[...].astype(BF16)
    copies[2].wait()
    taken[768:816, :] = coarse[:, 0:128]
    taken[816:864, :] = coarse[:, 128:256]
    copies[3].wait()


def pack_body(coarse, taken, weight, out):
    w = weight[...]
    own = (mm(coarse[...], w) * key_frame_present()).astype(BF16)
    before = (mm(taken[768:816, :], w[0:128, :]) + mm(taken[816:864, :], w[128:256, :])).astype(BF16)
    cots = jnp.concatenate([taken[912:928, :], jnp.zeros((16, 128), BF16)], axis=1)
    for band in range(N_ROWS):
        out[band, 0:48, :] = own
        out[band, 48:96, :] = before
        out[band, 96:112, :] = cots


def fine_body(taken, own, above, below, weight, first_out, mid_out, up_out, down_out, partial,
              first, queries, keys, key_grad, turned, window):
    scale = 1.0 / math.sqrt(128.0)
    w = weight[...]
    present = key_frame_present()
    queries[...] = mm(taken[0:768, :], w).astype(BF16).reshape(8, 96, 128)
    keys[:, 0:16, :] = jnp.zeros((16, 16, 128), BF16)
    keys[:, 112:128, :] = jnp.zeros((16, 16, 128), BF16)
    keys[0:4, 16:112, :] = (mm(above[...], w) * present).astype(BF16).reshape(4, 96, 128)
    keys[4:12, 16:112, :] = (mm(own[...], w) * present).astype(BF16).reshape(8, 96, 128)
    keys[12:16, 16:112, :] = (mm(below[...], w) * present).astype(BF16).reshape(4, 96, 128)
    key_grad[...] = jnp.zeros_like(key_grad)
    turned[...] = jnp.zeros_like(turned)
    terms = taken[864:912, :].astype(F32)
    refined = terms[0:16, :] + (terms[16:32, :] + terms[32:48, :])
    for k in range(6):
        turned[0:2, 128 * k : 128 * k + 128] = refined[2 * k : 2 * k + 2, :]
    upright = jnp.transpose(turned[...], (1, 0))
    lane = iota((1, 128), 1)
    query_x = jnp.bitwise_and(lane, 31).astype(F32)
    query_y = lax.shift_right_logical(lane, 5).astype(F32)
    key_x = iota((64, 128), 0).astype(F32) - 16.0
    near_x = jnp.where(jnp.abs(key_x - query_x) < 4.5, 0.0, -1e30)
    for line in range(12):
        near_y = jnp.where(jnp.abs(line - 4.0 - query_y) < 4.5, 0.0, -1e30)
        window[line] = jnp.minimum(near_x, near_y)
    for part in range(2):
        for column in range(3):
            q = queries[4 * part : 4 * part + 4, 32 * column : 32 * column + 32, :].reshape(128, 128)
            k = keys[4 * part : 4 * part + 12, 32 * column : 32 * column + 64, :].reshape(768, 128)
            pieces = [(4 * part + line) * 96 + 32 * column for line in range(4)]
            cot = jnp.transpose(jnp.concatenate([upright[at : at + 32, :] for at in pieces], axis=0), (1, 0))
            gx, gy = cot[0:1, :], cot[1:2, :]
            s = mm_nt(k, q).reshape(12, 64, 128) + window[...]
            top = jnp.max(jnp.max(s, axis=0), axis=0, keepdims=True)
            e = jnp.exp2((s - top) * (scale * math.log2(math.e)))
            by_x = jnp.sum(e, axis=0)
            inverse = 1.0 / jnp.sum(by_x, axis=0, keepdims=True)
            mean_x = jnp.sum(by_x * key_x, axis=0, keepdims=True) * inverse
            mean_y = jnp.zeros((1, 128), F32)
            for line in range(12):
                mean_y = mean_y + (line - 4.0) * jnp.sum(e[line], axis=0, keepdims=True)
            mean_y = mean_y * inverse
            factor = inverse * scale
            gx, gy = gx * factor, gy * factor
            bend_x = gx * (key_x - mean_x)
            weights = jnp.concatenate(
                [(e[line] * (bend_x + gy * ((line - 4.0) - mean_y))).astype(BF16) for line in range(12)], axis=0
            )
            first[4 * part : 4 * part + 4, 32 * column : 32 * column + 32, :] = mm_tn(weights, k).reshape(4, 32, 128)
            key_grad[4 * part : 4 * part + 12, 32 * column : 32 * column + 64, :] += mm(weights, q).reshape(12, 64, 128)
    up_out[...] = (key_grad[0:4, 16:112, :] * present).astype(BF16).reshape(384, 128)
    mid_out[...] = (key_grad[4:12, 16:112, :] * present).astype(BF16).reshape(768, 128)
    down_out[...] = (key_grad[12:16, 16:112, :] * present).astype(BF16).reshape(384, 128)
    exact = first[...].reshape(768, 128)
    hi = exact.astype(BF16)
    low = (exact - hi.astype(F32)).astype(BF16)
    first_out[...] = exact
    total = mm_tn(taken[0:768, :], hi) + mm_tn(taken[0:768, :], low)
    total = total + mm_tn(own[...], mid_out[...])
    partial[...] = total + mm_tn(above[...], up_out[...]) + mm_tn(below[...], down_out[...])


def match(scores, cot_x, cot_y):
    e = jnp.exp2((scores - jnp.max(scores, axis=0, keepdims=True)) * (math.log2(math.e) / 16.0)).reshape(16, 24, 384)
    by_x = jnp.sum(e, axis=0)
    inverse = 1.0 / jnp.sum(by_x, axis=0, keepdims=True)
    key_x = iota((24, 384), 0).astype(F32)
    mean_x = jnp.sum(by_x * key_x, axis=0, keepdims=True) * inverse
    mean_y = jnp.zeros((1, 384), F32)
    for line in range(1, 16):
        mean_y = mean_y + float(line) * jnp.sum(e[line], axis=0, keepdims=True)
    mean_y = mean_y * inverse
    factor = inverse * (1.0 / 16.0)
    cot_x, cot_y = cot_x * factor, cot_y * factor
    bend_x = cot_x * (key_x - mean_x)
    lines = [e[line] * (bend_x + cot_y * (float(line) - mean_y)) for line in range(16)]
    return jnp.concatenate(lines, axis=0).astype(BF16)


def coarse_body(bands, coarse, taken, fine_partial, fine_first, second, joined, send,
                sums_first, sums_second, packed):
    band, present = lax.axis_index("x") * 2 + lax.axis_index("yl"), key_frame_present()
    qa = bands[:, 48:96, :].reshape(384, 256)
    qb = bands[:, 0:48, :].reshape(384, 256)
    flat = jnp.zeros((16, 384), F32)
    ahead = iota((128, 384), 1) - iota((128, 384), 0)
    for source in range(N_ROWS):
        place = (ahead == 48 * source).astype(F32).astype(BF16)
        flat = flat + mm(bands[source, 96:112, 0:128], place)
    cots = flat[0:4, :] + (flat[4:8, :] + flat[8:12, :])
    forward_t = match(mm_nt(qb, qa), cots[0:1, :], cots[1:2, :])
    backward_t = match(mm_nt(qa, qb), cots[2:3, :], cots[3:4, :])
    sums_first[...] = mm_tn(forward_t, qb) + mm(backward_t, qb)
    sums_second[...] = mm(forward_t, qa) + mm_tn(backward_t, qa)
    mine = pl.ds(pl.multiple_of(band * 48, 16), 48)
    own_first = sums_first[mine, :]
    own_second = (sums_second[mine, :] * present).astype(BF16)
    second[...] = own_second
    hi = own_first.astype(BF16)
    low = (own_first - hi.astype(F32)).astype(BF16)
    joined[0:768, :] = fine_first[...]
    joined[768:816, :] = own_first[:, 0:128]
    joined[816:864, :] = own_first[:, 128:256]
    f_before = jnp.concatenate([taken[768:816, :], taken[816:864, :]], axis=1)
    total = mm_tn(f_before, hi) + mm_tn(f_before, low) + mm_tn(coarse[...], own_second)
    packed[:, 0:8, :] = total[:, 0:128].reshape(N_PLANE, 8, 128)
    packed[:, 8:16, :] = total[:, 128:256].reshape(N_PLANE, 8, 128)
    for chunk in range(N_PLANE):
        packed[chunk, 16:20, :] = fine_partial[4 * chunk : 4 * chunk + 4, :]
    send[...] = packed[...][:, 0:20, :].astype(BF16)


def sum_body(parts, out):
    total = parts[0].astype(F32)
    for source in range(1, parts.shape[0]):
        total = total + parts[source].astype(F32)
    rounded = total.astype(BF16)
    for target in range(out.shape[0]):
        out[target] = rounded


def unpack_body(parts, coarse, fine):
    values = parts[...].astype(F32) * (1.0 / N_FRAMES)
    coarse[:, 0:128] = values[:, 0:8, :].reshape(256, 128)
    coarse[:, 128:256] = values[:, 8:16, :].reshape(256, 128)
    for chunk in range(N_PLANE):
        fine[4 * chunk : 4 * chunk + 4, :] = values[chunk, 16:20, :]


def finish_body(returned, middle, from_above, from_below, weight, coarse_second, coarse_weight, fine_out, coarse_out):
    w = weight[...]
    total = returned[0:768, :] + middle[...].astype(F32)
    top = (total[0:384, :] + from_above[...].astype(F32)).astype(BF16)
    bottom = (total[384:768, :] + from_below[...].astype(F32)).astype(BF16)
    fine_out[0:384, :] = mm_nt(top, w).astype(BF16)
    fine_out[384:768, :] = mm_nt(bottom, w).astype(BF16)
    w = coarse_weight[...]
    second = coarse_second[...].astype(F32)
    left = (returned[768:816, :] + second[:, 0:128]).astype(BF16)
    right = (returned[816:864, :] + second[:, 128:256]).astype(BF16)
    coarse_out[...] = (mm_nt(left, w[:, 0:128]) + mm_nt(right, w[:, 128:256])).astype(BF16)


def shifted(value, frames, rows):
    pairs = [
        (f * N_ROWS + r, (f + frames) % N_FRAMES * N_ROWS + r + rows)
        for f in range(N_FRAMES)
        for r in range(max(0, -rows), min(N_ROWS, N_ROWS - rows))
    ]
    return lax.ppermute(value, ALL, pairs)


def local(coarse_features, fine_features, coarse_weight, fine_weight, grad_refined, grad_back):
    coarse_own = coarse_features.reshape(48, 256)
    fine_own = fine_features.reshape(768, 128)
    taken = call(
        prepare_body,
        shape(928, 128),
        [
            pltpu.VMEM((64, 128), F32),
            pltpu.VMEM((48, 256), BF16),
            pltpu.VMEM((2, 768), F32),
            pltpu.VMEM((2, 48), F32),
            pltpu.SemaphoreType.DMA((4,)),
        ],
        n_in=4, flops=10**9, nbytes=10**6, kind=HBM, room=60,
    )(coarse_own, fine_own, grad_refined.reshape(2, 768), grad_back.reshape(2, 48))
    rims = fine_own
    taken = shifted(taken, 1, 0)
    above = shifted(rims[384:768], 0, 1)
    below = shifted(rims[0:384], 0, -1)
    outgoing = call(pack_body, shape(N_ROWS, 112, 256), n_in=3, nbytes=10**6)(coarse_own, taken, coarse_weight)
    bands = lax.all_to_all(outgoing, ROWS, 0, 0, tiled=True)
    fine_first, middle, up_out, down_out, fine_partial = call(
        fine_body,
        (shape(768, 128, dtype=F32), shape(768, 128), shape(384, 128), shape(384, 128), shape(128, 128, dtype=F32)),
        [
            pltpu.VMEM((8, 96, 128), F32),
            pltpu.VMEM((8, 96, 128), BF16),
            pltpu.VMEM((16, 128, 128), BF16),
            pltpu.VMEM((16, 128, 128), F32),
            pltpu.VMEM((8, 768), F32),
            pltpu.VMEM((12, 64, 128), F32),
        ],
        n_in=5, flops=20 * 10**9, nbytes=4 * 10**6,
    )(taken, fine_own, above, below, fine_weight)
    back_up = shifted(up_out, 0, -1)
    back_down = shifted(down_out, 0, 1)
    coarse_second, joined, send = call(
        coarse_body,
        (shape(48, 256), shape(864, 128, dtype=F32), shape(N_PLANE, 20, 128)),
        [
            pltpu.VMEM((384, 256), F32),
            pltpu.VMEM((384, 256), F32),
            pltpu.VMEM((N_PLANE, 24, 128), F32),
        ],
        n_in=5, flops=3 * 10**9, nbytes=2 * 10**6,
    )(bands, coarse_own, taken, fine_partial, fine_first)
    returned = shifted(joined, -1, 0)
    parts = lax.all_to_all(send, PLANE, 0, 0, axis_index_groups=[[(28 + i) % N_PLANE for i in range(N_PLANE)]], tiled=True)
    copies = call(sum_body, shape(N_Z, 20, 128), n_in=1, nbytes=10**6)(parts)
    parts = lax.all_to_all(copies, "z", 0, 0, axis_index_groups=[[(9 + i) % N_Z for i in range(N_Z)]], tiled=True)
    copies = call(sum_body, shape(N_PLANE, 20, 128), n_in=1, nbytes=10**6)(parts)
    parts = lax.all_to_all(copies, PLANE, 0, 0, axis_index_groups=[[(28 + i) % N_PLANE for i in range(N_PLANE)]], tiled=True)
    coarse_total, fine_total = call(
        unpack_body, (shape(256, 256, dtype=F32), shape(128, 128, dtype=F32)), n_in=1, nbytes=10**6
    )(parts)
    fine_grad, coarse_grad = call(
        finish_body, (shape(768, 128), shape(48, 256)), n_in=7, flops=20 * 10**9, nbytes=10**6
    )(returned, middle, back_down, back_up, fine_weight, coarse_second, coarse_weight)
    return (
        coarse_grad.reshape(coarse_features.shape),
        fine_grad.reshape(fine_features.shape),
        coarse_total,
        fine_total,
    )


def solution(mesh):
    fine_mesh = Mesh(mesh.devices.reshape(16, 2, 2, 4, 2), ALL)
    in_specs = (
        P(FRAMES, ROWS, None, None),
        P(FRAMES, ROWS, None, None),
        P(),
        P(),
        P(FRAMES, None, ROWS),
        P(FRAMES, None, ROWS),
    )
    out_specs = (P(FRAMES, ROWS, None, None), P(FRAMES, ROWS, None, None), P(), P())
    return jax.shard_map(local, mesh=fine_mesh, in_specs=in_specs, out_specs=out_specs, check_vma=False)
```
